32 devices in a mesh: section: 4 (over y, core), seq: 8 (over z, x).
Axes of the slice: x: 2, y: 2, z: 4, core: 2. Of those that a mesh axis runs over, the one named last changes fastest.
Arguments:
- queries: bfloat16 [4, 2, 1024, 4096], P('section', None, 'seq'), may hold values from -20 to 20
- keys_values: bfloat16 [4, 2, 1024, 8, 256], P('section', None, 'seq'), may hold values from -20 to 20
- lengths: int32 [4, 2, 4], P('section'), may hold values from 1 to 512, 1024 in all within a row
- order: int32 [4, 2], P('section'), may hold values from 0 to 1, each once within a row
Outputs:
- handoff: bfloat16 [4, 2, 1024, 4096], P('section', None, 'seq')
The draws below stay inside these ranges and needn't reach their ends.
Inputs may be any that keep to these rules, and one draw needn't show every extreme that they name: Each row holds the lengths of 4 documents packed end to end, summing to 1024, the longest exactly 512. `order`: each row is a permutation of the microbatch numbers.
All inputs are finite; a program needn't handle non-finite values.
Results may differ from the reference program's by a relative error of at most 0.0037.
Values may be sent and summed in bfloat16 or wider, within the bound.
A program may use at most 64 MiB of HBM per device.

```python
import math
import jax
import jax.numpy as jnp
import numpy as np
from jax import lax

HD = 128
QH = 32
KVH = 8
MB = 2
DOCS = 4
TOKENS = 1024
DOC_MAX = 512
SECTIONS = 4


def draw_common(key):
    streams = jax.random.split(jax.random.fold_in(key, 7), 3)
    query_shape = (SECTIONS, MB, TOKENS, QH, HD)
    pair_shape = (SECTIONS, MB, TOKENS, KVH, HD)
    query_part = jax.random.truncated_normal(streams[0], -4.0, 4.0, query_shape, jnp.float32)
    key_part = jax.random.truncated_normal(streams[1], -4.0, 4.0, pair_shape, jnp.float32)
    value_part = jax.random.truncated_normal(streams[2], -4.0, 4.0, pair_shape, jnp.float32)
    return (query_part.reshape(SECTIONS, MB, TOKENS, QH * HD), jnp.concatenate([key_part, value_part], axis=-1))


def draw_queries(key, part):
    return draw_common(key)[0].astype(jnp.bfloat16)


def draw_keys_values(key, part):
    return draw_common(key)[1].astype(jnp.bfloat16)


def profile(number_of, total, reach, slope):
    loads = [(1 << 20) // math.isqrt(grade ** slope) + 1 for grade in range(2, number_of + 1)]
    surplus, holding = total - reach - (number_of - 1), [1] * (number_of - 1)
    while surplus > 0:
        candidates = [i for i in range(number_of - 1) if holding[i] < reach]
        whole, remaining = sum([loads[i] for i in candidates]), surplus
        for i in candidates:
            more = min(reach - holding[i], max(1, remaining * loads[i] // whole), surplus)
            holding[i] = holding[i] + more
            surplus = surplus - more
    return np.array([reach] + holding)


def uneven_parts(key, count, total, bound, skew):
    if count == 2:
        one = jax.random.randint(key, (), max(1, total - bound), min(bound, total - 1) + 1)
        return jnp.stack([one, total - one])
    tallies = jnp.asarray(profile(count, total, bound, skew), jnp.int32)
    couples = (count - 1) // 2
    giver, receiver = tallies[1:1 + 2 * couples:2], tallies[2:2 + 2 * couples:2]
    margin = jnp.minimum(giver - 1, bound - receiver)
    shifted = jax.random.randint(jax.random.fold_in(key, 1), (couples,), 0, 1 << 20) % (margin + 1)
    tallies = tallies.at[1:1 + 2 * couples:2].set(giver - shifted).at[2:2 + 2 * couples:2].set(receiver + shifted)
    return tallies[jax.random.permutation(jax.random.fold_in(key, 2), count)]


def setup_inputs(seed: int = 0) -> dict:
    key_list = jax.random.split(jax.random.key(seed), 5)
    return {
        "queries": draw_queries(jax.random.fold_in(key_list[4], 71), 0),
        "keys_values": draw_keys_values(jax.random.fold_in(key_list[4], 71), 0),
        "lengths": jax.vmap(lambda own: uneven_parts(own, DOCS, TOKENS, DOC_MAX, 2))(jax.random.split(key_list[2], SECTIONS * MB)).reshape((SECTIONS, MB, DOCS)).astype(jnp.int32),
        "order": jax.vmap(lambda own: jax.random.permutation(own, MB))(jax.random.split(key_list[3], SECTIONS)).reshape((SECTIONS, MB)).astype(jnp.int32),
    }


def segment_ids(lengths_row, rows_all):
    ends = jnp.cumsum(lengths_row).astype(jnp.int32)
    position = jnp.arange(rows_all, dtype=jnp.int32)
    return jnp.sum((position[:, None] >= ends[None, :]).astype(jnp.int32), axis=1).astype(jnp.int32)


def attend_one(operands):
    query_rows, pair_rows, lengths_row = operands
    rows_all = query_rows.shape[0]
    segment = segment_ids(lengths_row, rows_all)
    position = jnp.arange(rows_all, dtype=jnp.int32)
    allowed = (segment[:, None] == segment[None, :]) & (position[None, :] <= position[:, None])
    share = QH // KVH
    head_queries = jnp.transpose(query_rows.reshape(rows_all, QH, HD).astype(jnp.float32), (1, 0, 2))
    pairs = pair_rows.astype(jnp.float32)
    head_keys = jnp.repeat(jnp.transpose(pairs[:, :, :HD], (1, 0, 2)), share, axis=0)
    head_values = jnp.repeat(jnp.transpose(pairs[:, :, HD:], (1, 0, 2)), share, axis=0)

    def one_head(inputs):
        query_head, key_head, value_head = inputs
        scores = jnp.dot(query_head, key_head.T, precision=lax.Precision.HIGHEST) * (HD ** -0.5)
        peaks = jnp.max(jnp.where(allowed, scores, -jnp.inf), axis=1, keepdims=True)
        weights = jnp.where(allowed, jnp.exp(scores - peaks), jnp.float32(0.0))
        totals = jnp.sum(weights, axis=1, keepdims=True)
        rounded = lax.optimization_barrier(weights.astype(jnp.bfloat16)).astype(jnp.float32)
        mixed = jnp.dot(rounded, value_head, precision=lax.Precision.HIGHEST) / totals
        return mixed.astype(jnp.bfloat16)

    contexts = lax.map(one_head, (head_queries, head_keys, head_values))
    return jnp.transpose(contexts, (1, 0, 2)).reshape(rows_all, QH * HD)


def reference(queries, keys_values, lengths, order):
    flat_queries = queries.reshape(SECTIONS * MB, TOKENS, QH * HD)
    flat_pairs = keys_values.reshape(SECTIONS * MB, TOKENS, KVH, 2 * HD)
    flat_lengths = lengths.reshape(SECTIONS * MB, DOCS)
    contexts = lax.map(attend_one, (flat_queries, flat_pairs, flat_lengths))
    contexts = contexts.reshape(SECTIONS, MB, TOKENS, QH * HD)
    picked = jnp.take_along_axis(contexts, order[:, :, None, None].astype(jnp.int32), axis=1)
    return jnp.roll(picked, 1, axis=0)
```

```python
import math

import jax
import jax.numpy as jnp
from jax import lax
from jax.experimental import pallas as pl
from jax.experimental.pallas import tpu as pltpu
from jax.sharding import PartitionSpec as P

MESH = pl.DeviceIdType.MESH
LEAD = 3
MASKED = -1e30


def row_width(count):
    return max(w for w in range(1, count + 1) if count % w == 0 and w * w <= count)


def kernel(
    lengths_ref,
    order_ref,
    q_hbm,
    kv_hbm,
    out_hbm,
    kvbuf,
    qbuf,
    obuf,
    bias,
    local_sem,
    recv_sem,
    column_sem,
    row_sem,
    osend_sem,
    orecv_sem,
):
    n = lax.axis_size("seq")
    sections = lax.axis_size("section")
    width = row_width(n)
    depth = n // width
    reach = n // 2
    hops = -(-reach // width)
    micro, tok, q_cols = qbuf.shape
    chunks, keys, pair = kvbuf.shape
    head = pair // 2
    groups = chunks // micro
    out_cols = q_cols // groups
    share = out_cols // head
    docs = lengths_ref.shape[2]

    me = lax.axis_index("seq")
    section = lax.axis_index("section")
    x = me % width
    z = me // width
    row_moves = [
        (k, dx)
        for k in range(hops + 1)
        for dx in range(1 - width, width)
        if dx != 0 and 1 <= k * width + dx <= reach
    ]

    def slot(c, d):
        return kvbuf.at[c, pl.ds(d * tok, tok), :]

    def source(c, k):
        return kv_hbm.at[c] if k == 0 else slot(c, k * width)

    def column_copy(c, k):
        return pltpu.make_async_remote_copy(
            src_ref=source(c, k),
            dst_ref=slot(c, (k + 1) * width),
            send_sem=column_sem.at[k, c],
            recv_sem=recv_sem.at[(k + 1) * width, c],
            device_id=(section, me + width),
            device_id_type=MESH,
        )

    def row_copy(c, index):
        k, dx = row_moves[index]
        return pltpu.make_async_remote_copy(
            src_ref=source(c, k),
            dst_ref=slot(c, k * width + dx),
            send_sem=row_sem.at[index, c],
            recv_sem=recv_sem.at[k * width + dx, c],
            device_id=(section, me + dx),
            device_id_type=MESH,
        )

    def out_copy(c):
        columns = pl.ds(pl.multiple_of((c % groups) * out_cols, out_cols), out_cols)
        return pltpu.make_async_remote_copy(
            src_ref=obuf.at[c],
            dst_ref=out_hbm.at[0, c // groups, :, columns],
            send_sem=osend_sem.at[c],
            recv_sem=orecv_sem.at[c],
            device_id=((section + 1) % sections, me),
            device_id_type=MESH,
        )

    def each_send(c, k, act):
        if k < hops and (k + 1) * width <= reach:

            @pl.when((z + 1 < depth) & (z >= k))
            def _():
                act(column_copy(c, k))

        for index, (move_k, dx) in enumerate(row_moves):
            if move_k == k:

                @pl.when((x + dx >= 0) & (x + dx < width) & (z >= k))
                def _(index=index):
                    act(row_copy(c, index))

    def start_sends(c, k):
        each_send(c, k, lambda copy: copy.start())

    def arrived(c, d):
        @pl.when(me >= d)
        def _():
            pltpu.make_async_copy(slot(c, d), slot(c, d), recv_sem.at[d, c]).wait()

    barrier = pltpu.get_barrier_semaphore()

    def greet(condition, target):
        @pl.when(condition)
        def _():
            pl.semaphore_signal(barrier, inc=1, device_id=target, device_id_type=MESH)

    greet(z > 0, (section, me - width))
    greet(z + 1 < depth, (section, me + width))
    for dx in range(1 - width, width):
        if dx != 0:
            greet((x + dx >= 0) & (x + dx < width), (section, me + dx))
    for step in (1, sections - 1):
        greet(me >= 0, ((section + step) % sections, me))

    q_copy = pltpu.make_async_copy(q_hbm.at[0], qbuf, local_sem.at[0])
    kv_copy = pltpu.make_async_copy(kv_hbm, kvbuf.at[:, pl.ds(0, tok), :], local_sem.at[1])
    q_copy.start()
    kv_copy.start()

    for d in range(1, reach + 1):

        @pl.when(me < d)
        def _(d=d):
            def clear(c, carry):
                kvbuf[c, pl.ds(d * tok, tok), :] = jnp.zeros((tok, pair), kvbuf.dtype)
                return carry

            lax.fori_loop(0, chunks, clear, 0)

    for j in range(micro):
        m = order_ref[0, j]
        own = me * tok + lax.broadcasted_iota(jnp.int32, (tok, tok), 0)
        end = jnp.int32(0)
        begin = jnp.zeros((tok, tok), jnp.int32)
        for document in range(docs):
            end = end + lengths_ref[0, m, document]
            begin = jnp.where(own >= end, end, begin)
        for d in range(reach + 1):
            other = (me - d) * tok + lax.broadcasted_iota(jnp.int32, (tok, tok), 1)
            allowed = (other >= begin) & (other <= own)
            bias[j, :, pl.ds(d * tok, tok)] = jnp.where(allowed, 0.0, MASKED)

    column_mates = jnp.where(z > 0, 1, 0) + jnp.where(z + 1 < depth, 1, 0)
    pl.semaphore_wait(barrier, column_mates + (width - 1) + 2)

    lead = min(LEAD, chunks)
    for c in range(lead):
        start_sends(c, 0)
    q_copy.wait()
    kv_copy.wait()

    factor = head**-0.5 * math.log2(math.e)

    def compute(c):
        j = c // groups
        columns = pl.ds(pl.multiple_of((c % groups) * out_cols, out_cols), out_cols)
        q = qbuf[order_ref[0, j], :, columns]
        rows = jnp.concatenate([q[:, h * head : (h + 1) * head] for h in range(share)], axis=0)
        k = kvbuf[c, :, :head]
        v = kvbuf[c, :, head:]
        scores = lax.dot_general(
            rows, k, (((1,), (1,)), ((), ())), preferred_element_type=jnp.float32
        )
        hidden = bias[j]
        for h in range(share):
            part = scores[h * tok : (h + 1) * tok] * factor + hidden
            weights = jnp.exp2(part - jnp.max(part, axis=1, keepdims=True))
            totals = jnp.sum(weights, axis=1, keepdims=True)
            mixed = jnp.dot(weights.astype(jnp.bfloat16), v, preferred_element_type=jnp.float32)
            obuf[c, :, h * head : (h + 1) * head] = (mixed / totals).astype(obuf.dtype)

    def turn(t, carry):
        @pl.when(t + lead < chunks)
        def _():
            start_sends(t + lead, 0)

        for k in range(1, hops + 1):
            if k * width <= reach:

                @pl.when((t - (k - 1) >= 0) & (t - (k - 1) < chunks))
                def _(k=k):
                    arrived(t - (k - 1), k * width)
                    start_sends(t - (k - 1), k)

        @pl.when(t >= hops)
        def _():
            c = t - hops
            for d in range(1, reach + 1):
                if d % width != 0:
                    arrived(c, d)
            compute(c)
            out_copy(c).start()

        return carry

    lax.fori_loop(0, chunks + hops, turn, 0)

    def drain(c, carry):
        for k in range(hops + 1):
            each_send(c, k, lambda copy: copy.wait_send())
        out_copy(c).wait()
        return carry

    lax.fori_loop(0, chunks, drain, 0)


def local(queries, keys_values, lengths, order):
    n = lax.axis_size("seq")
    width = row_width(n)
    reach = n // 2
    hops = -(-reach // width)
    _, micro, tok, q_cols = queries.shape
    groups, pair = keys_values.shape[3:]
    chunks = micro * groups
    out_cols = q_cols // groups
    moves = sum(
        1
        for k in range(hops + 1)
        for dx in range(1 - width, width)
        if dx != 0 and 1 <= k * width + dx <= reach
    )

    picked = []
    for j in range(micro):
        one = keys_values[0, 0]
        for m in range(1, micro):
            one = jnp.where(order[0, j] == m, keys_values[0, m], one)
        picked.append(one)
    pairs = jnp.stack(picked).transpose(0, 2, 1, 3).reshape(chunks, tok, pair)

    keys = (reach + 1) * tok
    return pl.pallas_call(
        kernel,
        out_shape=jax.ShapeDtypeStruct(queries.shape, queries.dtype),
        in_specs=[
            pl.BlockSpec(memory_space=pltpu.SMEM),
            pl.BlockSpec(memory_space=pltpu.SMEM),
            pl.BlockSpec(memory_space=pl.ANY),
            pl.BlockSpec(memory_space=pl.ANY),
        ],
        out_specs=pl.BlockSpec(memory_space=pl.ANY),
        scratch_shapes=[
            pltpu.VMEM((chunks, keys, pair), jnp.bfloat16),
            pltpu.VMEM((micro, tok, q_cols), jnp.bfloat16),
            pltpu.VMEM((chunks, tok, out_cols), jnp.bfloat16),
            pltpu.VMEM((micro, tok, keys), jnp.float32),
            pltpu.SemaphoreType.DMA((2,)),
            pltpu.SemaphoreType.DMA((reach + 1, chunks)),
            pltpu.SemaphoreType.DMA((hops, chunks)),
            pltpu.SemaphoreType.DMA((max(1, moves), chunks)),
            pltpu.SemaphoreType.DMA((chunks,)),
            pltpu.SemaphoreType.DMA((chunks,)),
        ],
        compiler_params=pltpu.CompilerParams(
            collective_id=0,
            has_side_effects=True,
            vmem_limit_bytes=48 * 1024 * 1024,
        ),
        name="relay_attention",
    )(lengths, order, queries, pairs)


def solution(mesh):
    placed = (
        P("section", None, "seq", None),
        P("section", None, "seq", None, None),
        P("section", None, None),
        P("section", None),
    )
    return jax.shard_map(
        local,
        mesh=mesh,
        in_specs=placed,
        out_specs=P("section", None, "seq", None),
        check_vma=False,
    )
```

```python
import math

import jax
import jax.numpy as jnp
from jax import lax
from jax.experimental import pallas as pl
from jax.experimental.pallas import tpu as pltpu
from jax.sharding import PartitionSpec as P

MESH = pl.DeviceIdType.MESH
LEAD = 3
MASKED = -1e30


def row_width(count):
    return max(w for w in range(1, count + 1) if count % w == 0 and w * w <= count)


def kernel(
    lengths_ref,
    order_ref,
    q_hbm,
    kv_hbm,
    out_hbm,
    raw,
    spread,
    kvbuf,
    qbuf,
    obuf,
    bias,
    local_sem,
    recv_sem,
    column_sem,
    row_sem,
    osend_sem,
    orecv_sem,
):
    n = lax.axis_size("seq")
    sections = lax.axis_size("section")
    width = row_width(n)
    depth = n // width
    reach = n // 2
    hops = -(-reach // width)
    micro, tok, q_cols = qbuf.shape
    chunks, keys, pair = kvbuf.shape
    head = pair // 2
    groups = chunks // micro
    out_cols = q_cols // groups
    share = out_cols // head
    parts, part_cols = obuf.shape[1], obuf.shape[3]
    part_heads = part_cols // head
    docs = lengths_ref.shape[2]

    me = lax.axis_index("seq")
    section = lax.axis_index("section")
    x = me % width
    z = me // width
    row_moves = [
        (k, dx)
        for k in range(hops + 1)
        for dx in range(1 - width, width)
        if dx != 0 and 1 <= k * width + dx <= reach
    ]

    def slot(c, d):
        return kvbuf.at[c, pl.ds(d * tok, tok), :]

    def column_copy(c, k):
        return pltpu.make_async_remote_copy(
            src_ref=slot(c, k * width),
            dst_ref=slot(c, (k + 1) * width),
            send_sem=column_sem.at[k, c],
            recv_sem=recv_sem.at[(k + 1) * width, c],
            device_id=(section, me + width),
            device_id_type=MESH,
        )

    def row_copy(c, index):
        k, dx = row_moves[index]
        return pltpu.make_async_remote_copy(
            src_ref=slot(c, k * width),
            dst_ref=slot(c, k * width + dx),
            send_sem=row_sem.at[index, c],
            recv_sem=recv_sem.at[k * width + dx, c],
            device_id=(section, me + dx),
            device_id_type=MESH,
        )

    def out_copy(c, part):
        first = pl.multiple_of((c % groups) * out_cols + part * part_cols, part_cols)
        return pltpu.make_async_remote_copy(
            src_ref=obuf.at[c, part],
            dst_ref=out_hbm.at[0, c // groups, :, pl.ds(first, part_cols)],
            send_sem=osend_sem.at[part, c],
            recv_sem=orecv_sem.at[part, c],
            device_id=((section + 1) % sections, me),
            device_id_type=MESH,
        )

    def each_send(c, k, act):
        if k < hops and (k + 1) * width <= reach:

            @pl.when((z + 1 < depth) & (z >= k))
            def _():
                act(column_copy(c, k))

        for index, (move_k, dx) in enumerate(row_moves):
            if move_k == k:

                @pl.when((x + dx >= 0) & (x + dx < width) & (z >= k))
                def _(index=index):
                    act(row_copy(c, index))

    def start_sends(c, k):
        each_send(c, k, lambda copy: copy.start())

    def arrived(c, d):
        @pl.when(me >= d)
        def _():
            pltpu.make_async_copy(slot(c, d), slot(c, d), recv_sem.at[d, c]).wait()

    barrier = pltpu.get_barrier_semaphore()

    def greet(condition, target):
        @pl.when(condition)
        def _():
            pl.semaphore_signal(barrier, inc=1, device_id=target, device_id_type=MESH)

    greet(z > 0, (section, me - width))
    greet(z + 1 < depth, (section, me + width))
    for dx in range(1 - width, width):
        if dx != 0:
            greet((x + dx >= 0) & (x + dx < width), (section, me + dx))
    for step in (1, sections - 1):
        greet(me >= 0, ((section + step) % sections, me))

    kv_copies = [
        pltpu.make_async_copy(kv_hbm.at[0, m], raw.at[m], local_sem.at[1 + m]) for m in range(micro)
    ]
    q_copy = pltpu.make_async_copy(q_hbm.at[0], qbuf, local_sem.at[0])
    for copy in kv_copies:
        copy.start()
    q_copy.start()
    for copy in kv_copies:
        copy.wait()

    def by_head(j):
        for half in range(2):
            columns = pl.ds(half * head, head)
            one = raw[order_ref[0, j], :, :, columns]
            spread[half] = one.astype(jnp.float32).reshape(tok * groups, head)
            for g in range(groups):
                kvbuf[j * groups + g, pl.ds(0, tok), columns] = spread[
                    half, pl.ds(g, tok, stride=groups), :
                ].astype(kvbuf.dtype)

    lead = min(LEAD, groups)
    by_head(0)
    column_mates = jnp.where(z > 0, 1, 0) + jnp.where(z + 1 < depth, 1, 0)
    pl.semaphore_wait(barrier, column_mates + (width - 1) + 2)
    for c in range(lead):
        start_sends(c, 0)
    for j in range(1, micro):
        by_head(j)

    for d in range(1, reach + 1):

        @pl.when(me < d)
        def _(d=d):
            def clear(c, carry):
                kvbuf[c, pl.ds(d * tok, tok), :] = jnp.zeros((tok, pair), kvbuf.dtype)
                return carry

            lax.fori_loop(0, chunks, clear, 0)

    for j in range(micro):
        m = order_ref[0, j]
        own = me * tok + lax.broadcasted_iota(jnp.int32, (tok, tok), 0)
        end = jnp.int32(0)
        begin = jnp.zeros((tok, tok), jnp.int32)
        for document in range(docs):
            end = end + lengths_ref[0, m, document]
            begin = jnp.where(own >= end, end, begin)
        for d in range(reach + 1):
            other = (me - d) * tok + lax.broadcasted_iota(jnp.int32, (tok, tok), 1)
            allowed = (other >= begin) & (other <= own)
            bias[j, :, pl.ds(d * tok, tok)] = jnp.where(allowed, 0.0, MASKED)

    q_copy.wait()
    factor = head**-0.5 * math.log2(math.e)

    def compute(c):
        j = c // groups
        k = kvbuf[c, :, :head]
        v = kvbuf[c, :, head:]
        hidden = bias[j]
        for part in range(parts):
            first = pl.multiple_of((c % groups) * out_cols + part * part_cols, part_cols)
            q = qbuf[order_ref[0, j], :, pl.ds(first, part_cols)]
            rows = jnp.concatenate(
                [q[:, h * head : (h + 1) * head] for h in range(part_heads)], axis=0
            )
            scores = lax.dot_general(
                rows, k, (((1,), (1,)), ((), ())), preferred_element_type=jnp.float32
            )
            for h in range(part_heads):
                logits = scores[h * tok : (h + 1) * tok] * factor + hidden
                weights = jnp.exp2(logits - jnp.max(logits, axis=1, keepdims=True))
                totals = jnp.sum(weights, axis=1, keepdims=True)
                mixed = jnp.dot(
                    weights.astype(jnp.bfloat16), v, preferred_element_type=jnp.float32
                )
                obuf[c, part, :, h * head : (h + 1) * head] = (mixed / totals).astype(obuf.dtype)
            out_copy(c, part).start()

    def turn(t, carry):
        @pl.when(t + lead < chunks)
        def _():
            start_sends(t + lead, 0)

        for k in range(1, hops + 1):
            if k * width <= reach:

                @pl.when((t - (k - 1) >= 0) & (t - (k - 1) < chunks))
                def _(k=k):
                    arrived(t - (k - 1), k * width)
                    start_sends(t - (k - 1), k)

        @pl.when(t >= hops)
        def _():
            c = t - hops
            for d in range(1, reach + 1):
                if d % width != 0:
                    arrived(c, d)
            compute(c)

        return carry

    lax.fori_loop(0, chunks + hops, turn, 0)

    def drain(c, carry):
        for k in range(hops + 1):
            each_send(c, k, lambda copy: copy.wait_send())
        for part in range(parts):
            out_copy(c, part).wait()
        return carry

    lax.fori_loop(0, chunks, drain, 0)


def local(queries, keys_values, lengths, order):
    n = lax.axis_size("seq")
    width = row_width(n)
    reach = n // 2
    hops = -(-reach // width)
    _, micro, tok, q_cols = queries.shape
    groups, pair = keys_values.shape[3:]
    chunks = micro * groups
    out_cols = q_cols // groups
    moves = sum(
        1
        for k in range(hops + 1)
        for dx in range(1 - width, width)
        if dx != 0 and 1 <= k * width + dx <= reach
    )

    parts = 2 if (out_cols // (pair // 2)) % 2 == 0 else 1
    keys = (reach + 1) * tok
    return pl.pallas_call(
        kernel,
        out_shape=jax.ShapeDtypeStruct(queries.shape, queries.dtype),
        in_specs=[
            pl.BlockSpec(memory_space=pltpu.SMEM),
            pl.BlockSpec(memory_space=pltpu.SMEM),
            pl.BlockSpec(memory_space=pltpu.HBM),
            pl.BlockSpec(memory_space=pltpu.HBM),
        ],
        out_specs=pl.BlockSpec(memory_space=pl.ANY),
        scratch_shapes=[
            pltpu.VMEM((micro, tok, groups, pair), jnp.bfloat16),
            pltpu.VMEM((2, tok * groups, pair // 2), jnp.float32),
            pltpu.VMEM((chunks, keys, pair), jnp.bfloat16),
            pltpu.VMEM((micro, tok, q_cols), jnp.bfloat16),
            pltpu.VMEM((chunks, parts, tok, out_cols // parts), jnp.bfloat16),
            pltpu.VMEM((micro, tok, keys), jnp.float32),
            pltpu.SemaphoreType.DMA((1 + micro,)),
            pltpu.SemaphoreType.DMA((reach + 1, chunks)),
            pltpu.SemaphoreType.DMA((hops, chunks)),
            pltpu.SemaphoreType.DMA((max(1, moves), chunks)),
            pltpu.SemaphoreType.DMA((parts, chunks)),
            pltpu.SemaphoreType.DMA((parts, chunks)),
        ],
        compiler_params=pltpu.CompilerParams(
            collective_id=0,
            has_side_effects=True,
            vmem_limit_bytes=60 * 1024 * 1024,
        ),
        name="relay_attention",
    )(lengths, order, queries, keys_values)


def solution(mesh):
    placed = (
        P("section", None, "seq", None),
        P("section", None, "seq", None, None),
        P("section", None, None),
        P("section", None),
    )
    return jax.shard_map(
        local,
        mesh=mesh,
        in_specs=placed,
        out_specs=P("section", None, "seq", None),
        check_vma=False,
    )
```

```python
import math

import jax
import jax.numpy as jnp
from jax import lax
from jax.experimental import pallas as pl
from jax.experimental.pallas import tpu as pltpu
from jax.sharding import PartitionSpec as P

MESH = pl.DeviceIdType.MESH
LEAD = 3
MASKED = -1e30


def row_width(count):
    return max(w for w in range(1, count + 1) if count % w == 0 and w * w <= count)


def kernel(
    lengths_ref,
    order_ref,
    q_hbm,
    kv_hbm,
    out_hbm,
    raw,
    spread,
    kvbuf,
    qbuf,
    obuf,
    bias,
    local_sem,
    recv_sem,
    column_sem,
    row_sem,
    osend_sem,
    orecv_sem,
):
    n = lax.axis_size("seq")
    sections = lax.axis_size("section")
    width = row_width(n)
    depth = n // width
    reach = n // 2
    hops = -(-reach // width)
    micro, tok, q_cols = qbuf.shape
    pieces = recv_sem.shape[1]
    rows = tok // pieces
    chunks, keys, pair = kvbuf.shape
    head = pair // 2
    groups = chunks // micro
    out_cols = q_cols // groups
    share = out_cols // head
    joint = 2 if share % 2 == 0 else 1
    docs = lengths_ref.shape[2]

    me = lax.axis_index("seq")
    section = lax.axis_index("section")
    x = me % width
    z = me // width
    row_moves = [
        (k, dx)
        for k in range(hops + 1)
        for dx in range(1 - width, width)
        if dx != 0 and 1 <= k * width + dx <= reach
    ]

    def slot(c, d, p):
        return kvbuf.at[c, pl.ds(d * tok + p * rows, rows), :]

    def column_copy(c, k, p):
        return pltpu.make_async_remote_copy(
            src_ref=slot(c, k * width, p),
            dst_ref=slot(c, (k + 1) * width, p),
            send_sem=column_sem.at[k, p, c],
            recv_sem=recv_sem.at[(k + 1) * width, p, c],
            device_id=(section, me + width),
            device_id_type=MESH,
        )

    def row_copy(c, index, p):
        k, dx = row_moves[index]
        return pltpu.make_async_remote_copy(
            src_ref=slot(c, k * width, p),
            dst_ref=slot(c, k * width + dx, p),
            send_sem=row_sem.at[index, p, c],
            recv_sem=recv_sem.at[k * width + dx, p, c],
            device_id=(section, me + dx),
            device_id_type=MESH,
        )

    def out_copy(c, h):
        first = pl.multiple_of((c % groups) * out_cols + h * head, head)
        return pltpu.make_async_remote_copy(
            src_ref=obuf.at[c, h],
            dst_ref=out_hbm.at[0, c // groups, :, pl.ds(first, head)],
            send_sem=osend_sem.at[h, c],
            recv_sem=orecv_sem.at[h, c],
            device_id=((section + 1) % sections, me),
            device_id_type=MESH,
        )

    def each_send(c, k, p, act):
        if k < hops and (k + 1) * width <= reach:

            @pl.when((z + 1 < depth) & (z >= k))
            def _():
                act(column_copy(c, k, p))

        for index, (move_k, dx) in enumerate(row_moves):
            if move_k == k:

                @pl.when((x + dx >= 0) & (x + dx < width) & (z >= k))
                def _(index=index):
                    act(row_copy(c, index, p))

    def start_sends(c, k, p):
        each_send(c, k, p, lambda copy: copy.start())

    def arrived(c, d, p):
        @pl.when(me >= d)
        def _():
            pltpu.make_async_copy(slot(c, d, p), slot(c, d, p), recv_sem.at[d, p, c]).wait()

    barrier = pltpu.get_barrier_semaphore()

    def greet(condition, target):
        @pl.when(condition)
        def _():
            pl.semaphore_signal(barrier, inc=1, device_id=target, device_id_type=MESH)

    greet(z > 0, (section, me - width))
    greet(z + 1 < depth, (section, me + width))
    for dx in range(1 - width, width):
        if dx != 0:
            greet((x + dx >= 0) & (x + dx < width), (section, me + dx))
    for step in (1, sections - 1):
        greet(me >= 0, ((section + step) % sections, me))

    kv_copies = [
        pltpu.make_async_copy(kv_hbm.at[0, m], raw.at[m], local_sem.at[1 + m]) for m in range(micro)
    ]
    q_copy = pltpu.make_async_copy(q_hbm.at[0], qbuf, local_sem.at[0])
    for copy in kv_copies:
        copy.start()
    q_copy.start()
    for copy in kv_copies:
        copy.wait()

    def by_head(j):
        for half in range(2):
            columns = pl.ds(half * head, head)
            one = raw[order_ref[0, j], :, :, columns]
            spread[half] = one.astype(jnp.float32).reshape(tok * groups, head)
            for g in range(groups):
                kvbuf[j * groups + g, pl.ds(0, tok), columns] = spread[
                    half, pl.ds(g, tok, stride=groups), :
                ].astype(kvbuf.dtype)

    lead = min(LEAD, groups)
    by_head(0)
    column_mates = jnp.where(z > 0, 1, 0) + jnp.where(z + 1 < depth, 1, 0)
    pl.semaphore_wait(barrier, column_mates + (width - 1) + 2)
    for c in range(lead):
        for p in range(pieces):
            start_sends(c, 0, p)
    for j in range(1, micro):
        by_head(j)

    for d in range(1, reach + 1):

        @pl.when(me < d)
        def _(d=d):
            def clear(c, carry):
                kvbuf[c, pl.ds(d * tok, tok), :] = jnp.zeros((tok, pair), kvbuf.dtype)
                return carry

            lax.fori_loop(0, chunks, clear, 0)

    for j in range(micro):
        m = order_ref[0, j]
        own = me * tok + lax.broadcasted_iota(jnp.int32, (tok, tok), 0)
        end = jnp.int32(0)
        begin = jnp.zeros((tok, tok), jnp.int32)
        for document in range(docs):
            end = end + lengths_ref[0, m, document]
            begin = jnp.where(own >= end, end, begin)
        for d in range(reach + 1):
            other = (me - d) * tok + lax.broadcasted_iota(jnp.int32, (tok, tok), 1)
            allowed = (other >= begin) & (other <= own)
            bias[j, :, pl.ds(d * tok, tok)] = jnp.where(allowed, 0.0, MASKED)

    q_copy.wait()
    factor = head**-0.5 * math.log2(math.e)

    def compute(c):
        j = c // groups
        k = kvbuf[c, :, :head]
        v = kvbuf[c, :, head:]
        hidden = bias[j]
        for pair_first in range(0, share, joint):
            first = pl.multiple_of((c % groups) * out_cols + pair_first * head, joint * head)
            q = qbuf[order_ref[0, j], :, pl.ds(first, joint * head)]
            stacked = jnp.concatenate(
                [q[:, i * head : (i + 1) * head] for i in range(joint)], axis=0
            )
            scores = lax.dot_general(
                stacked, k, (((1,), (1,)), ((), ())), preferred_element_type=jnp.float32
            )
            for i in range(joint):
                logits = scores[i * tok : (i + 1) * tok] * factor + hidden
                weights = jnp.exp2(logits - jnp.max(logits, axis=1, keepdims=True))
                totals = jnp.sum(weights, axis=1, keepdims=True)
                mixed = jnp.dot(
                    weights.astype(jnp.bfloat16), v, preferred_element_type=jnp.float32
                )
                obuf[c, pair_first + i] = (mixed / totals).astype(obuf.dtype)
                out_copy(c, pair_first + i).start()

    def turn(t, carry):
        @pl.when(t + lead < chunks)
        def _():
            for p in range(pieces):
                start_sends(t + lead, 0, p)

        for k in range(1, hops + 1):
            if k * width <= reach:

                @pl.when((t - (k - 1) >= 0) & (t - (k - 1) < chunks))
                def _(k=k):
                    for p in range(pieces):
                        arrived(t - (k - 1), k * width, p)
                        start_sends(t - (k - 1), k, p)

        @pl.when(t >= hops)
        def _():
            c = t - hops
            for d in range(1, reach + 1):
                if d % width != 0:
                    for p in range(pieces):
                        arrived(c, d, p)
            compute(c)

        return carry

    lax.fori_loop(0, chunks + hops, turn, 0)

    def drain(c, carry):
        for k in range(hops + 1):
            for p in range(pieces):
                each_send(c, k, p, lambda copy: copy.wait_send())
        for h in range(share):
            out_copy(c, h).wait()
        return carry

    lax.fori_loop(0, chunks, drain, 0)


def local(queries, keys_values, lengths, order):
    n = lax.axis_size("seq")
    width = row_width(n)
    reach = n // 2
    hops = -(-reach // width)
    _, micro, tok, q_cols = queries.shape
    groups, pair = keys_values.shape[3:]
    chunks = micro * groups
    out_cols = q_cols // groups
    moves = sum(
        1
        for k in range(hops + 1)
        for dx in range(1 - width, width)
        if dx != 0 and 1 <= k * width + dx <= reach
    )

    head = pair // 2
    share = out_cols // head
    pieces = 2 if tok % 32 == 0 else 1
    keys = (reach + 1) * tok
    inputs = [pltpu.with_memory_space_constraint(a, pltpu.HBM) for a in (queries, keys_values)]
    return pl.pallas_call(
        kernel,
        out_shape=jax.ShapeDtypeStruct(queries.shape, queries.dtype),
        in_specs=[
            pl.BlockSpec(memory_space=pltpu.SMEM),
            pl.BlockSpec(memory_space=pltpu.SMEM),
            pl.BlockSpec(memory_space=pltpu.HBM),
            pl.BlockSpec(memory_space=pltpu.HBM),
        ],
        out_specs=pl.BlockSpec(memory_space=pl.ANY),
        scratch_shapes=[
            pltpu.VMEM((micro, tok, groups, pair), jnp.bfloat16),
            pltpu.VMEM((2, tok * groups, pair // 2), jnp.float32),
            pltpu.VMEM((chunks, keys, pair), jnp.bfloat16),
            pltpu.VMEM((micro, tok, q_cols), jnp.bfloat16),
            pltpu.VMEM((chunks, share, tok, head), jnp.bfloat16),
            pltpu.VMEM((micro, tok, keys), jnp.float32),
            pltpu.SemaphoreType.DMA((1 + micro,)),
            pltpu.SemaphoreType.DMA((reach + 1, pieces, chunks)),
            pltpu.SemaphoreType.DMA((hops, pieces, chunks)),
            pltpu.SemaphoreType.DMA((max(1, moves), pieces, chunks)),
            pltpu.SemaphoreType.DMA((share, chunks)),
            pltpu.SemaphoreType.DMA((share, chunks)),
        ],
        compiler_params=pltpu.CompilerParams(
            collective_id=0,
            has_side_effects=True,
            vmem_limit_bytes=40 * 1024 * 1024,
        ),
        name="relay_attention",
    )(lengths, order, *inputs)


def solution(mesh):
    placed = (
        P("section", None, "seq", None),
        P("section", None, "seq", None, None),
        P("section", None, None),
        P("section", None),
    )
    return jax.shard_map(
        local,
        mesh=mesh,
        in_specs=placed,
        out_specs=P("section", None, "seq", None),
        check_vma=False,
    )
```

```python
import math

import jax
import jax.numpy as jnp
from jax import lax
from jax.experimental import pallas as pl
from jax.experimental.pallas import tpu as pltpu
from jax.sharding import PartitionSpec as P

MESH = pl.DeviceIdType.MESH
LEAD = 3
MASKED = -1e30


def row_width(count):
    return max(w for w in range(1, count + 1) if count % w == 0 and w * w <= count)


def kernel(
    lengths_ref,
    order_ref,
    q_hbm,
    kv_hbm,
    out_hbm,
    raw,
    spread,
    kvbuf,
    qbuf,
    obuf,
    bias,
    local_sem,
    recv_sem,
    column_sem,
    row_sem,
    osend_sem,
    orecv_sem,
):
    n = lax.axis_size("seq")
    sections = lax.axis_size("section")
    width = row_width(n)
    depth = n // width
    reach = n // 2
    hops = -(-reach // width)
    micro, tok, q_cols = qbuf.shape
    pieces = recv_sem.shape[1]
    rows = tok // pieces
    chunks, keys, pair = kvbuf.shape
    head = pair // 2
    groups = chunks // micro
    out_cols = q_cols // groups
    share = out_cols // head
    parts, part_cols = obuf.shape[1], obuf.shape[3]
    joint = part_cols // head
    block = tok // 2
    docs = lengths_ref.shape[2]

    me = lax.axis_index("seq")
    section = lax.axis_index("section")
    x = me % width
    z = me // width
    row_moves = [
        (k, dx)
        for k in range(hops + 1)
        for dx in range(1 - width, width)
        if dx != 0 and 1 <= k * width + dx <= reach
    ]

    def slot(c, d, p):
        return kvbuf.at[c, pl.ds(d * tok + p * rows, rows), :]

    def column_copy(c, k, p):
        return pltpu.make_async_remote_copy(
            src_ref=slot(c, k * width, p),
            dst_ref=slot(c, (k + 1) * width, p),
            send_sem=column_sem.at[k, p, c],
            recv_sem=recv_sem.at[(k + 1) * width, p, c],
            device_id=(section, me + width),
            device_id_type=MESH,
        )

    def row_copy(c, index, p):
        k, dx = row_moves[index]
        return pltpu.make_async_remote_copy(
            src_ref=slot(c, k * width, p),
            dst_ref=slot(c, k * width + dx, p),
            send_sem=row_sem.at[index, p, c],
            recv_sem=recv_sem.at[k * width + dx, p, c],
            device_id=(section, me + dx),
            device_id_type=MESH,
        )

    def out_copy(c, part):
        first = pl.multiple_of((c % groups) * out_cols + part * part_cols, part_cols)
        return pltpu.make_async_remote_copy(
            src_ref=obuf.at[c, part],
            dst_ref=out_hbm.at[0, c // groups, :, pl.ds(first, part_cols)],
            send_sem=osend_sem.at[part, c],
            recv_sem=orecv_sem.at[part, c],
            device_id=((section + 1) % sections, me),
            device_id_type=MESH,
        )

    def each_send(c, k, p, act):
        if k < hops and (k + 1) * width <= reach:

            @pl.when((z + 1 < depth) & (z >= k))
            def _():
                act(column_copy(c, k, p))

        for index, (move_k, dx) in enumerate(row_moves):
            if move_k == k:

                @pl.when((x + dx >= 0) & (x + dx < width) & (z >= k))
                def _(index=index):
                    act(row_copy(c, index, p))

    def start_sends(c, k, p):
        each_send(c, k, p, lambda copy: copy.start())

    def arrived(c, d, p):
        @pl.when(me >= d)
        def _():
            pltpu.make_async_copy(slot(c, d, p), slot(c, d, p), recv_sem.at[d, p, c]).wait()

    barrier = pltpu.get_barrier_semaphore()

    def greet(condition, target):
        @pl.when(condition)
        def _():
            pl.semaphore_signal(barrier, inc=1, device_id=target, device_id_type=MESH)

    greet(z > 0, (section, me - width))
    greet(z + 1 < depth, (section, me + width))
    for dx in range(1 - width, width):
        if dx != 0:
            greet((x + dx >= 0) & (x + dx < width), (section, me + dx))
    for step in (1, sections - 1):
        greet(me >= 0, ((section + step) % sections, me))

    kv_copies = [
        pltpu.make_async_copy(kv_hbm.at[0, m], raw.at[m], local_sem.at[1 + m]) for m in range(micro)
    ]
    q_copy = pltpu.make_async_copy(q_hbm.at[0], qbuf, local_sem.at[0])
    for copy in kv_copies:
        copy.start()
    q_copy.start()
    for copy in kv_copies:
        copy.wait()

    def by_head(j):
        for half in range(2):
            columns = pl.ds(half * head, head)
            one = raw[order_ref[0, j], :, :, columns]
            spread[half] = one.astype(jnp.float32).reshape(tok * groups, head)
            for g in range(groups):
                kvbuf[j * groups + g, pl.ds(0, tok), columns] = spread[
                    half, pl.ds(g, tok, stride=groups), :
                ].astype(kvbuf.dtype)

    lead = min(LEAD, groups)
    by_head(0)
    column_mates = jnp.where(z > 0, 1, 0) + jnp.where(z + 1 < depth, 1, 0)
    pl.semaphore_wait(barrier, column_mates + (width - 1) + 2)
    for c in range(lead):
        for p in range(pieces):
            start_sends(c, 0, p)
    for j in range(1, micro):
        by_head(j)

    for d in range(1, reach + 1):

        @pl.when(me < d)
        def _(d=d):
            def clear(c, carry):
                kvbuf[c, pl.ds(d * tok, tok), :] = jnp.zeros((tok, pair), kvbuf.dtype)
                return carry

            lax.fori_loop(0, chunks, clear, 0)

    for j in range(micro):
        m = order_ref[0, j]
        own = me * tok + lax.broadcasted_iota(jnp.int32, (tok, tok), 0)
        end = jnp.int32(0)
        begin = jnp.zeros((tok, tok), jnp.int32)
        for document in range(docs):
            end = end + lengths_ref[0, m, document]
            begin = jnp.where(own >= end, end, begin)
        for d in range(reach + 1):
            other = (me - d) * tok + lax.broadcasted_iota(jnp.int32, (tok, tok), 1)
            allowed = (other >= begin) & (other <= own)
            bias[j, :, pl.ds(d * tok, tok)] = jnp.where(allowed, 0.0, MASKED)

    q_copy.wait()
    factor = head**-0.5 * math.log2(math.e)

    def compute(c):
        j = c // groups
        k = kvbuf[c, :, :head]
        v = jnp.concatenate([kvbuf[c, :, head:], jnp.ones((keys, head), kvbuf.dtype)], axis=1)
        for part in range(parts):
            first = pl.multiple_of((c % groups) * out_cols + part * part_cols, part_cols)
            q = qbuf[order_ref[0, j], :, pl.ds(first, part_cols)]
            stacked = jnp.concatenate(
                [q[:, i * head : (i + 1) * head] for i in range(joint)], axis=0
            )
            scores = lax.dot_general(
                stacked, k, (((1,), (1,)), ((), ())), preferred_element_type=jnp.float32
            )
            weights = []
            for top in range(0, joint * tok, block):
                hidden = bias[j, pl.ds(top % tok, block), :]
                logits = scores[top : top + block] * factor + hidden
                lifted = logits - jnp.max(logits, axis=1, keepdims=True)
                weights.append(jnp.exp2(lifted).astype(jnp.bfloat16))
            mixed = jnp.dot(
                jnp.concatenate(weights, axis=0), v, preferred_element_type=jnp.float32
            )
            result = (mixed[:, :head] / mixed[:, head:]).astype(obuf.dtype)
            for i in range(joint):
                obuf[c, part, :, i * head : (i + 1) * head] = result[i * tok : (i + 1) * tok]
            out_copy(c, part).start()

    def turn(t, carry):
        @pl.when(t + lead < chunks)
        def _():
            for p in range(pieces):
                start_sends(t + lead, 0, p)

        for k in range(1, hops + 1):
            if k * width <= reach:

                @pl.when((t - (k - 1) >= 0) & (t - (k - 1) < chunks))
                def _(k=k):
                    for p in range(pieces):
                        arrived(t - (k - 1), k * width, p)
                        start_sends(t - (k - 1), k, p)

        @pl.when(t >= hops)
        def _():
            c = t - hops
            for d in range(1, reach + 1):
                if d % width != 0:
                    for p in range(pieces):
                        arrived(c, d, p)
            compute(c)

        return carry

    lax.fori_loop(0, chunks + hops, turn, 0)

    def drain(c, carry):
        for k in range(hops + 1):
            for p in range(pieces):
                each_send(c, k, p, lambda copy: copy.wait_send())
        for part in range(parts):
            out_copy(c, part).wait()
        return carry

    lax.fori_loop(0, chunks, drain, 0)


def local(queries, keys_values, lengths, order):
    n = lax.axis_size("seq")
    width = row_width(n)
    reach = n // 2
    hops = -(-reach // width)
    _, micro, tok, q_cols = queries.shape
    groups, pair = keys_values.shape[3:]
    chunks = micro * groups
    out_cols = q_cols // groups
    moves = sum(
        1
        for k in range(hops + 1)
        for dx in range(1 - width, width)
        if dx != 0 and 1 <= k * width + dx <= reach
    )

    head = pair // 2
    share = out_cols // head
    joint = 2 if share % 2 == 0 else 1
    pieces = 1
    keys = (reach + 1) * tok
    inputs = [
        pltpu.with_memory_space_constraint(a, pltpu.HBM)
        for a in (lengths, order, queries, keys_values)
    ]
    return pl.pallas_call(
        kernel,
        out_shape=jax.ShapeDtypeStruct(queries.shape, queries.dtype),
        in_specs=[
            pl.BlockSpec(memory_space=pltpu.SMEM),
            pl.BlockSpec(memory_space=pltpu.SMEM),
            pl.BlockSpec(memory_space=pltpu.HBM),
            pl.BlockSpec(memory_space=pltpu.HBM),
        ],
        out_specs=pl.BlockSpec(memory_space=pl.ANY),
        scratch_shapes=[
            pltpu.VMEM((micro, tok, groups, pair), jnp.bfloat16),
            pltpu.VMEM((2, tok * groups, pair // 2), jnp.float32),
            pltpu.VMEM((chunks, keys, pair), jnp.bfloat16),
            pltpu.VMEM((micro, tok, q_cols), jnp.bfloat16),
            pltpu.VMEM((chunks, share // joint, tok, joint * head), jnp.bfloat16),
            pltpu.VMEM((micro, tok, keys), jnp.float32),
            pltpu.SemaphoreType.DMA((1 + micro,)),
            pltpu.SemaphoreType.DMA((reach + 1, pieces, chunks)),
            pltpu.SemaphoreType.DMA((hops, pieces, chunks)),
            pltpu.SemaphoreType.DMA((max(1, moves), pieces, chunks)),
            pltpu.SemaphoreType.DMA((share // joint, chunks)),
            pltpu.SemaphoreType.DMA((share // joint, chunks)),
        ],
        compiler_params=pltpu.CompilerParams(
            collective_id=0,
            has_side_effects=True,
            vmem_limit_bytes=40 * 1024 * 1024,
        ),
        name="relay_attention",
    )(*inputs)


def solution(mesh):
    placed = (
        P("section", None, "seq", None),
        P("section", None, "seq", None, None),
        P("section", None, None),
        P("section", None),
    )
    return jax.shard_map(
        local,
        mesh=mesh,
        in_specs=placed,
        out_specs=P("section", None, "seq", None),
        check_vma=False,
    )
```

```python
import math

import jax
import jax.numpy as jnp
from jax import lax
from jax.experimental import pallas as pl
from jax.experimental.pallas import tpu as pltpu
from jax.sharding import PartitionSpec as P

MESH = pl.DeviceIdType.MESH
LEAD = 3
MASKED = -1e30


def row_width(count):
    return max(w for w in range(1, count + 1) if count % w == 0 and w * w <= count)


def kernel(
    lengths_ref,
    order_ref,
    q_hbm,
    kv_hbm,
    out_hbm,
    raw,
    spread,
    kvbuf,
    qbuf,
    obuf,
    bias,
    local_sem,
    recv_sem,
    column_sem,
    row_sem,
    osend_sem,
    orecv_sem,
):
    n = lax.axis_size("seq")
    sections = lax.axis_size("section")
    width = row_width(n)
    depth = n // width
    reach = n // 2
    hops = -(-reach // width)
    micro, tok, q_cols = qbuf.shape
    chunks, keys, pair = kvbuf.shape
    head = pair // 2
    groups = chunks // micro
    out_cols = q_cols // groups
    share = out_cols // head
    parts, part_cols = obuf.shape[1], obuf.shape[3]
    joint = part_cols // head
    block = tok // 2
    docs = lengths_ref.shape[2]
    last = chunks - 1
    halves = 2 if tok % 32 == 0 else 1

    me = lax.axis_index("seq")
    section = lax.axis_index("section")
    x = me % width
    z = me // width
    row_moves = [
        (k, dx)
        for k in range(hops + 1)
        for dx in range(1 - width, width)
        if dx != 0 and 1 <= k * width + dx <= reach
    ]

    def slot(c, d, p):
        rows = tok if p is None else tok // halves
        return kvbuf.at[c, pl.ds(d * tok + (p or 0) * rows, rows), :]

    def arrival(c, d, p):
        return recv_sem.at[d, chunks if p == 1 else c]

    def column_copy(c, k, p):
        return pltpu.make_async_remote_copy(
            src_ref=slot(c, k * width, p),
            dst_ref=slot(c, (k + 1) * width, p),
            send_sem=column_sem.at[k],
            recv_sem=arrival(c, (k + 1) * width, p),
            device_id=(section, me + width),
            device_id_type=MESH,
        )

    def row_copy(c, index, p):
        k, dx = row_moves[index]
        return pltpu.make_async_remote_copy(
            src_ref=slot(c, k * width, p),
            dst_ref=slot(c, k * width + dx, p),
            send_sem=row_sem.at[index],
            recv_sem=arrival(c, k * width + dx, p),
            device_id=(section, me + dx),
            device_id_type=MESH,
        )

    def out_copy(c, part):
        first = pl.multiple_of((c % groups) * out_cols + part * part_cols, part_cols)
        return pltpu.make_async_remote_copy(
            src_ref=obuf.at[c, part],
            dst_ref=out_hbm.at[0, c // groups, :, pl.ds(first, part_cols)],
            send_sem=osend_sem,
            recv_sem=orecv_sem,
            device_id=((section + 1) % sections, me),
            device_id_type=MESH,
        )

    def by_piece(c, d, act):
        if d <= (hops - 1) * width:
            act(None)
            return

        @pl.when(c < last)
        def _():
            act(None)

        @pl.when(c == last)
        def _():
            for p in range(halves):
                act(p)

    def column_goes(k):
        return (z + 1 < depth) & (z >= k)

    def row_goes(index):
        k, dx = row_moves[index]
        return (x + dx >= 0) & (x + dx < width) & (z >= k)

    def each_send(k, act):
        if k < hops and (k + 1) * width <= reach:

            @pl.when(column_goes(k))
            def _():
                act(column_copy, k, (k + 1) * width)

        for index, (move_k, dx) in enumerate(row_moves):
            if move_k == k:

                @pl.when(row_goes(index))
                def _(index=index, dx=dx):
                    act(row_copy, index, k * width + dx)

    def start_sends(c, k, p=None):
        if p is None:
            each_send(k, lambda copy, i, d: by_piece(c, d, lambda q: copy(c, i, q).start()))
        else:
            each_send(k, lambda copy, i, d: copy(c, i, p).start())

    def arrived(c, d, p):
        @pl.when(me >= d)
        def _():
            pltpu.make_async_copy(slot(c, d, p), slot(c, d, p), arrival(c, d, p)).wait()

    def arrived_and_on(c, k):
        def act(p):
            arrived(c, k * width, p)
            start_sends(c, k, p)

        by_piece(c, k * width, act)

    barrier = pltpu.get_barrier_semaphore()

    def greet(condition, target):
        @pl.when(condition)
        def _():
            pl.semaphore_signal(barrier, inc=1, device_id=target, device_id_type=MESH)

    greet(z > 0, (section, me - width))
    greet(z + 1 < depth, (section, me + width))
    for dx in range(1 - width, width):
        if dx != 0:
            greet((x + dx >= 0) & (x + dx < width), (section, me + dx))
    for step in (1, sections - 1):
        greet(me >= 0, ((section + step) % sections, me))

    kv_copies = [
        pltpu.make_async_copy(kv_hbm.at[0, m], raw.at[m], local_sem.at[1 + m]) for m in range(micro)
    ]
    q_copy = pltpu.make_async_copy(q_hbm.at[0], qbuf, local_sem.at[0])
    for copy in kv_copies:
        copy.start()
    q_copy.start()
    for copy in kv_copies:
        copy.wait()

    def by_head(j, then):
        for half in range(2):
            one = raw[order_ref[0, j], :, :, pl.ds(half * head, head)]
            spread[half] = one.astype(jnp.float32).reshape(tok * groups, head)
        for g in range(groups):
            for half in range(2):
                kvbuf[j * groups + g, pl.ds(0, tok), pl.ds(half * head, head)] = spread[
                    half, pl.ds(g, tok, stride=groups), :
                ].astype(kvbuf.dtype)
            then(g)

    leads = [min(LEAD, groups), min(2, groups), 1]
    turns = [0, chunks // 2, chunks * 3 // 4, chunks]

    def first_sends(g):
        if g == 0:
            column_mates = jnp.where(z > 0, 1, 0) + jnp.where(z + 1 < depth, 1, 0)
            pl.semaphore_wait(barrier, column_mates + (width - 1) + 2)
        if g < leads[0]:
            start_sends(jnp.int32(g), 0)

    by_head(0, first_sends)
    for j in range(1, micro):
        by_head(j, lambda g: None)

    for d in range(1, reach + 1):

        @pl.when(me < d)
        def _(d=d):
            def clear(c, carry):
                kvbuf[c, pl.ds(d * tok, tok), :] = jnp.zeros((tok, pair), kvbuf.dtype)
                return carry

            lax.fori_loop(0, chunks, clear, 0)

    for j in range(micro):
        m = order_ref[0, j]
        own = me * tok + lax.broadcasted_iota(jnp.int32, (tok, tok), 0)
        end = jnp.int32(0)
        begin = jnp.zeros((tok, tok), jnp.int32)
        for document in range(docs):
            end = end + lengths_ref[0, m, document]
            begin = jnp.where(own >= end, end, begin)
        for d in range(reach + 1):
            other = (me - d) * tok + lax.broadcasted_iota(jnp.int32, (tok, tok), 1)
            allowed = (other >= begin) & (other <= own)
            bias[j, :, pl.ds(d * tok, tok)] = jnp.where(allowed, 0.0, MASKED)

    q_copy.wait()
    factor = head**-0.5 * math.log2(math.e)

    def compute(c):
        j = c // groups
        k = kvbuf[c, :, :head]
        v = jnp.concatenate([kvbuf[c, :, head:], jnp.ones((keys, head), kvbuf.dtype)], axis=1)
        for part in range(parts):
            first = pl.multiple_of((c % groups) * out_cols + part * part_cols, part_cols)
            q = qbuf[order_ref[0, j], :, pl.ds(first, part_cols)]
            stacked = jnp.concatenate(
                [q[:, i * head : (i + 1) * head] for i in range(joint)], axis=0
            )
            scores = lax.dot_general(
                stacked, k, (((1,), (1,)), ((), ())), preferred_element_type=jnp.float32
            )
            weights = []
            for top in range(0, joint * tok, block):
                hidden = bias[j, pl.ds(top % tok, block), :]
                logits = scores[top : top + block] * factor + hidden
                lifted = logits - jnp.max(logits, axis=1, keepdims=True)
                weights.append(jnp.exp2(lifted).astype(jnp.bfloat16))
            mixed = jnp.dot(
                jnp.concatenate(weights, axis=0), v, preferred_element_type=jnp.float32
            )
            result = (mixed[:, :head] / mixed[:, head:]).astype(obuf.dtype)
            for i in range(joint):
                obuf[c, part, :, i * head : (i + 1) * head] = result[i * tok : (i + 1) * tok]
            out_copy(c, part).start()

    def turn(t, carry):
        for lead, begin, end in zip(leads, turns, turns[1:]):
            begin = max(begin, leads[0])

            @pl.when((t + lead >= begin) & (t + lead < end))
            def _(lead=lead):
                start_sends(t + lead, 0)

        for k in range(1, hops + 1):
            if k * width <= reach:

                @pl.when((t - (k - 1) >= 0) & (t - (k - 1) < chunks))
                def _(k=k):
                    arrived_and_on(t - (k - 1), k)

        @pl.when(t >= hops)
        def _():
            c = t - hops
            for d in range(1, reach + 1):
                if d % width != 0:
                    by_piece(c, d, lambda p, d=d: arrived(c, d, p))
            compute(c)

        return carry

    lax.fori_loop(0, chunks + hops, turn, 0)

    def sent(ref, sem):
        pltpu.make_async_copy(ref, ref, sem).wait()

    def drained(k):
        return kvbuf.at[:, pl.ds(k * width * tok, tok), :]

    for k in range(hops):
        if (k + 1) * width <= reach:

            @pl.when(column_goes(k))
            def _(k=k):
                sent(drained(k), column_sem.at[k])

    for index, (k, _) in enumerate(row_moves):

        @pl.when(row_goes(index))
        def _(k=k, index=index):
            sent(drained(k), row_sem.at[index])

    sent(obuf, osend_sem)
    sent(out_hbm.at[0], orecv_sem)


def local(queries, keys_values, lengths, order):
    n = lax.axis_size("seq")
    width = row_width(n)
    reach = n // 2
    hops = -(-reach // width)
    _, micro, tok, q_cols = queries.shape
    groups, pair = keys_values.shape[3:]
    chunks = micro * groups
    out_cols = q_cols // groups
    moves = sum(
        1
        for k in range(hops + 1)
        for dx in range(1 - width, width)
        if dx != 0 and 1 <= k * width + dx <= reach
    )

    head = pair // 2
    share = out_cols // head
    joint = 2 if share % 2 == 0 else 1
    keys = (reach + 1) * tok
    inputs = [
        pltpu.with_memory_space_constraint(a, pltpu.HBM)
        for a in (lengths, order, queries, keys_values)
    ]
    return pl.pallas_call(
        kernel,
        out_shape=jax.ShapeDtypeStruct(queries.shape, queries.dtype),
        in_specs=[
            pl.BlockSpec(memory_space=pltpu.SMEM),
            pl.BlockSpec(memory_space=pltpu.SMEM),
            pl.BlockSpec(memory_space=pltpu.HBM),
            pl.BlockSpec(memory_space=pltpu.HBM),
        ],
        out_specs=pl.BlockSpec(memory_space=pl.ANY),
        scratch_shapes=[
            pltpu.VMEM((micro, tok, groups, pair), jnp.bfloat16),
            pltpu.VMEM((2, tok * groups, pair // 2), jnp.float32),
            pltpu.VMEM((chunks, keys, pair), jnp.bfloat16),
            pltpu.VMEM((micro, tok, q_cols), jnp.bfloat16),
            pltpu.VMEM((chunks, share // joint, tok, joint * head), jnp.bfloat16),
            pltpu.VMEM((micro, tok, keys), jnp.float32),
            pltpu.SemaphoreType.DMA((1 + micro,)),
            pltpu.SemaphoreType.DMA((reach + 1, chunks + 1)),
            pltpu.SemaphoreType.DMA((hops,)),
            pltpu.SemaphoreType.DMA((max(1, moves),)),
            pltpu.SemaphoreType.DMA(()),
            pltpu.SemaphoreType.DMA(()),
        ],
        compiler_params=pltpu.CompilerParams(
            collective_id=0,
            has_side_effects=True,
            vmem_limit_bytes=40 * 1024 * 1024,
        ),
        name="relay_attention",
    )(*inputs)


def solution(mesh):
    placed = (
        P("section", None, "seq", None),
        P("section", None, "seq", None, None),
        P("section", None, None),
        P("section", None),
    )
    return jax.shard_map(
        local,
        mesh=mesh,
        in_specs=placed,
        out_specs=P("section", None, "seq", None),
        check_vma=False,
    )
```

```python
import math

import jax
import jax.numpy as jnp
from jax import lax
from jax.experimental import pallas as pl
from jax.experimental.pallas import tpu as pltpu
from jax.sharding import PartitionSpec as P

MESH = pl.DeviceIdType.MESH
LEAD = 3
MASKED = -1e30


def row_width(count):
    return max(w for w in range(1, count + 1) if count % w == 0 and w * w <= count)


def kernel(
    lengths_ref,
    order_ref,
    q_hbm,
    kv_hbm,
    out_hbm,
    raw,
    spread,
    kvbuf,
    qbuf,
    obuf,
    bias,
    local_sem,
    recv_sem,
    column_sem,
    row_sem,
    osend_sem,
    orecv_sem,
):
    n = lax.axis_size("seq")
    sections = lax.axis_size("section")
    width = row_width(n)
    depth = n // width
    reach = n // 2
    hops = -(-reach // width)
    micro, tok, q_cols = qbuf.shape
    chunks, keys, pair = kvbuf.shape
    head = pair // 2
    groups = chunks // micro
    out_cols = q_cols // groups
    share = out_cols // head
    parts, part_cols = obuf.shape[1], obuf.shape[3]
    joint = part_cols // head
    block = tok // 2
    docs = lengths_ref.shape[2]
    last = chunks - 1
    halves = 2 if tok % 32 == 0 else 1

    me = lax.axis_index("seq")
    section = lax.axis_index("section")
    x = me % width
    z = me // width
    row_moves = [
        (k, dx)
        for k in range(hops + 1)
        for dx in range(1 - width, width)
        if dx != 0 and 1 <= k * width + dx <= reach
    ]

    def slot(c, d, p):
        rows = tok if p is None else tok // halves
        return kvbuf.at[c, pl.ds(d * tok + (p or 0) * rows, rows), :]

    def arrival(c, d, p):
        return recv_sem.at[d, chunks if p == 1 else c]

    def column_copy(c, k, p):
        return pltpu.make_async_remote_copy(
            src_ref=slot(c, k * width, p),
            dst_ref=slot(c, (k + 1) * width, p),
            send_sem=column_sem.at[k],
            recv_sem=arrival(c, (k + 1) * width, p),
            device_id=(section, me + width),
            device_id_type=MESH,
        )

    def row_copy(c, index, p):
        k, dx = row_moves[index]
        return pltpu.make_async_remote_copy(
            src_ref=slot(c, k * width, p),
            dst_ref=slot(c, k * width + dx, p),
            send_sem=row_sem.at[index],
            recv_sem=arrival(c, k * width + dx, p),
            device_id=(section, me + dx),
            device_id_type=MESH,
        )

    def out_copy(c, part):
        first = pl.multiple_of((c % groups) * out_cols + part * part_cols, part_cols)
        return pltpu.make_async_remote_copy(
            src_ref=obuf.at[c, part],
            dst_ref=out_hbm.at[0, c // groups, :, pl.ds(first, part_cols)],
            send_sem=osend_sem,
            recv_sem=orecv_sem,
            device_id=((section + 1) % sections, me),
            device_id_type=MESH,
        )

    def by_piece(c, d, act):
        if d <= (hops - 1) * width:
            act(None)
            return

        @pl.when(c < last)
        def _():
            act(None)

        @pl.when(c == last)
        def _():
            for p in range(halves):
                act(p)

    def column_goes(k):
        return (z + 1 < depth) & (z >= k)

    def row_goes(index):
        k, dx = row_moves[index]
        return (x + dx >= 0) & (x + dx < width) & (z >= k)

    def each_send(k, act):
        if k < hops and (k + 1) * width <= reach:

            @pl.when(column_goes(k))
            def _():
                act(column_copy, k, (k + 1) * width)

        for index, (move_k, dx) in enumerate(row_moves):
            if move_k == k:

                @pl.when(row_goes(index))
                def _(index=index, dx=dx):
                    act(row_copy, index, k * width + dx)

    def start_sends(c, k, p=None):
        if p is None:
            each_send(k, lambda copy, i, d: by_piece(c, d, lambda q: copy(c, i, q).start()))
        else:
            each_send(k, lambda copy, i, d: copy(c, i, p).start())

    def arrived(c, d, p):
        @pl.when(me >= d)
        def _():
            pltpu.make_async_copy(slot(c, d, p), slot(c, d, p), arrival(c, d, p)).wait()

    def arrived_and_on(c, k):
        def act(p):
            arrived(c, k * width, p)
            start_sends(c, k, p)

        by_piece(c, k * width, act)

    barrier = pltpu.get_barrier_semaphore()

    def greet(condition, target):
        @pl.when(condition)
        def _():
            pl.semaphore_signal(barrier, inc=1, device_id=target, device_id_type=MESH)

    greet(z > 0, (section, me - width))
    greet(z + 1 < depth, (section, me + width))
    for dx in range(1 - width, width):
        if dx != 0:
            greet((x + dx >= 0) & (x + dx < width), (section, me + dx))
    for step in (1, sections - 1):
        greet(me >= 0, ((section + step) % sections, me))

    kv_copies = [
        pltpu.make_async_copy(kv_hbm.at[0, m], raw.at[m], local_sem.at[1 + m]) for m in range(micro)
    ]
    q_copy = pltpu.make_async_copy(q_hbm.at[0], qbuf, local_sem.at[0])
    for copy in kv_copies:
        copy.start()
    q_copy.start()
    for copy in kv_copies:
        copy.wait()

    def by_head(j, then):
        for half in range(2):
            one = raw[order_ref[0, j], :, :, pl.ds(half * head, head)]
            spread[half] = one.astype(jnp.float32).reshape(tok * groups, head)
        for g in range(groups):
            for half in range(2):
                kvbuf[j * groups + g, pl.ds(0, tok), pl.ds(half * head, head)] = spread[
                    half, pl.ds(g, tok, stride=groups), :
                ].astype(kvbuf.dtype)
            then(g)

    leads = [min(LEAD, groups), min(2, groups), 1]
    turns = [0, chunks // 2, chunks * 3 // 4, chunks]

    def first_sends(g):
        if g == 0:
            column_mates = jnp.where(z > 0, 1, 0) + jnp.where(z + 1 < depth, 1, 0)
            pl.semaphore_wait(barrier, column_mates + (width - 1) + 2)
        if g < leads[0]:
            start_sends(jnp.int32(g), 0)

    by_head(0, first_sends)
    for j in range(1, micro):
        by_head(j, lambda g: None)

    for d in range(1, reach + 1):

        @pl.when(me < d)
        def _(d=d):
            def clear(c, carry):
                kvbuf[c, pl.ds(d * tok, tok), :] = jnp.zeros((tok, pair), kvbuf.dtype)
                return carry

            lax.fori_loop(0, chunks, clear, 0)

    for j in range(micro):
        m = order_ref[0, j]
        own = me * tok + lax.broadcasted_iota(jnp.int32, (tok, tok), 0)
        end = jnp.int32(0)
        begin = jnp.zeros((tok, tok), jnp.int32)
        for document in range(docs):
            end = end + lengths_ref[0, m, document]
            begin = jnp.where(own >= end, end, begin)
        for d in range(reach + 1):
            other = (me - d) * tok + lax.broadcasted_iota(jnp.int32, (tok, tok), 1)
            allowed = (other >= begin) & (other <= own)
            bias[j, :, pl.ds(d * tok, tok)] = jnp.where(allowed, 0.0, MASKED)

    q_copy.wait()
    factor = head**-0.5 * math.log2(math.e)

    def compute(c, turn_parts):
        j = c // groups
        k = kvbuf[c, :, :head]
        v = jnp.concatenate([kvbuf[c, :, head:], jnp.ones((keys, head), kvbuf.dtype)], axis=1)
        for part in turn_parts:
            first = pl.multiple_of((c % groups) * out_cols + part * part_cols, part_cols)
            q = qbuf[order_ref[0, j], :, pl.ds(first, part_cols)]
            stacked = jnp.concatenate(
                [q[:, i * head : (i + 1) * head] for i in range(joint)], axis=0
            )
            scores = lax.dot_general(
                stacked, k, (((1,), (1,)), ((), ())), preferred_element_type=jnp.float32
            )
            weights = []
            for top in range(0, joint * tok, block):
                hidden = bias[j, pl.ds(top % tok, block), :]
                logits = scores[top : top + block] * factor + hidden
                lifted = logits - jnp.max(logits, axis=1, keepdims=True)
                weights.append(jnp.exp2(lifted).astype(jnp.bfloat16))
            mixed = jnp.dot(
                jnp.concatenate(weights, axis=0), v, preferred_element_type=jnp.float32
            )
            result = (mixed[:, :head] / mixed[:, head:]).astype(obuf.dtype)
            for i in range(joint):
                obuf[c, part, :, i * head : (i + 1) * head] = result[i * tok : (i + 1) * tok]
            out_copy(c, part).start()

    def turn(t, carry):
        for lead, begin, end in zip(leads, turns, turns[1:]):
            begin = max(begin, leads[0])

            @pl.when((t + lead >= begin) & (t + lead < end))
            def _(lead=lead):
                start_sends(t + lead, 0)

        for k in range(1, hops + 1):
            if k * width <= reach:

                @pl.when((t - (k - 1) >= 0) & (t - (k - 1) < chunks))
                def _(k=k):
                    arrived_and_on(t - (k - 1), k)

            @pl.when(t >= hops)
            def _(k=k):
                c = t - hops
                if k == 1:
                    for d in range(1, reach + 1):
                        if d % width != 0:
                            by_piece(c, d, lambda p, d=d: arrived(c, d, p))
                compute(c, range((k - 1) * parts // hops, k * parts // hops))

        return carry

    lax.fori_loop(0, chunks + hops, turn, 0)

    def sent(ref, sem):
        pltpu.make_async_copy(ref, ref, sem).wait()

    def drained(k):
        return kvbuf.at[:, pl.ds(k * width * tok, tok), :]

    for k in range(hops):
        if (k + 1) * width <= reach:

            @pl.when(column_goes(k))
            def _(k=k):
                sent(drained(k), column_sem.at[k])

    for index, (k, _) in enumerate(row_moves):

        @pl.when(row_goes(index))
        def _(k=k, index=index):
            sent(drained(k), row_sem.at[index])

    sent(obuf, osend_sem)
    sent(out_hbm.at[0], orecv_sem)


def local(queries, keys_values, lengths, order):
    n = lax.axis_size("seq")
    width = row_width(n)
    reach = n // 2
    hops = -(-reach // width)
    _, micro, tok, q_cols = queries.shape
    groups, pair = keys_values.shape[3:]
    chunks = micro * groups
    out_cols = q_cols // groups
    moves = sum(
        1
        for k in range(hops + 1)
        for dx in range(1 - width, width)
        if dx != 0 and 1 <= k * width + dx <= reach
    )

    head = pair // 2
    share = out_cols // head
    joint = 2 if share % 2 == 0 else 1
    keys = (reach + 1) * tok
    inputs = [
        pltpu.with_memory_space_constraint(a, pltpu.HBM)
        for a in (lengths, order, queries, keys_values)
    ]
    return pl.pallas_call(
        kernel,
        out_shape=jax.ShapeDtypeStruct(queries.shape, queries.dtype),
        in_specs=[
            pl.BlockSpec(memory_space=pltpu.SMEM),
            pl.BlockSpec(memory_space=pltpu.SMEM),
            pl.BlockSpec(memory_space=pltpu.HBM),
            pl.BlockSpec(memory_space=pltpu.HBM),
        ],
        out_specs=pl.BlockSpec(memory_space=pl.ANY),
        scratch_shapes=[
            pltpu.VMEM((micro, tok, groups, pair), jnp.bfloat16),
            pltpu.VMEM((2, tok * groups, pair // 2), jnp.float32),
            pltpu.VMEM((chunks, keys, pair), jnp.bfloat16),
            pltpu.VMEM((micro, tok, q_cols), jnp.bfloat16),
            pltpu.VMEM((chunks, share // joint, tok, joint * head), jnp.bfloat16),
            pltpu.VMEM((micro, tok, keys), jnp.float32),
            pltpu.SemaphoreType.DMA((1 + micro,)),
            pltpu.SemaphoreType.DMA((reach + 1, chunks + 1)),
            pltpu.SemaphoreType.DMA((hops,)),
            pltpu.SemaphoreType.DMA((max(1, moves),)),
            pltpu.SemaphoreType.DMA(()),
            pltpu.SemaphoreType.DMA(()),
        ],
        compiler_params=pltpu.CompilerParams(
            collective_id=0,
            has_side_effects=True,
            vmem_limit_bytes=40 * 1024 * 1024,
        ),
        name="relay_attention",
    )(*inputs)


def solution(mesh):
    placed = (
        P("section", None, "seq", None),
        P("section", None, "seq", None, None),
        P("section", None, None),
        P("section", None),
    )
    return jax.shard_map(
        local,
        mesh=mesh,
        in_specs=placed,
        out_specs=P("section", None, "seq", None),
        check_vma=False,
    )
```

```python
import math

import jax
import jax.numpy as jnp
from jax import lax
from jax.experimental import pallas as pl
from jax.experimental.pallas import tpu as pltpu
from jax.sharding import PartitionSpec as P

MESH = pl.DeviceIdType.MESH
LEAD = 3
PERIOD = 8
MASKED = -1e30


def row_width(count):
    return max(w for w in range(1, count + 1) if count % w == 0 and w * w <= count)


def kernel(
    lengths_ref,
    order_ref,
    q_hbm,
    kv_hbm,
    out_hbm,
    raw,
    spread,
    kvbuf,
    qbuf,
    obuf,
    bias,
    local_sem,
    recv_sem,
    column_sem,
    row_sem,
    straight_sem,
    osend_sem,
    orecv_sem,
):
    n = lax.axis_size("seq")
    sections = lax.axis_size("section")
    width = row_width(n)
    depth = n // width
    reach = n // 2
    hops = -(-reach // width)
    micro, tok, q_cols = qbuf.shape
    chunks, keys, pair = kvbuf.shape
    head = pair // 2
    groups = chunks // micro
    out_cols = q_cols // groups
    share = out_cols // head
    parts, part_cols = obuf.shape[1], obuf.shape[3]
    joint = part_cols // head
    block = tok // 2
    docs = lengths_ref.shape[2]
    last = chunks - 1
    halves = 2 if tok % 32 == 0 else 1

    me = lax.axis_index("seq")
    section = lax.axis_index("section")
    x = me % width
    z = me // width
    row_moves = [
        (k, dx)
        for k in range(hops + 1)
        for dx in range(1 - width, width)
        if dx != 0 and 1 <= k * width + dx <= reach
    ]

    straight = hops * width - 1
    eased = row_moves.index((hops, -1)) if (hops, -1) in row_moves and straight > width else None
    straight_count = chunks // PERIOD if eased is not None else 0

    def goes_straight(c):
        return c % PERIOD == PERIOD // 2 - 1

    def straight_goes():
        return (x + 1 < width) & (z + 1 < depth) & (z + 1 >= hops)

    def slot(c, d, p):
        rows = tok if p is None else tok // halves
        return kvbuf.at[c, pl.ds(d * tok + (p or 0) * rows, rows), :]

    def arrival(c, d, p):
        return recv_sem.at[d, chunks if p == 1 else c]

    def column_copy(c, k, p):
        return pltpu.make_async_remote_copy(
            src_ref=slot(c, k * width, p),
            dst_ref=slot(c, (k + 1) * width, p),
            send_sem=column_sem.at[k],
            recv_sem=arrival(c, (k + 1) * width, p),
            device_id=(section, me + width),
            device_id_type=MESH,
        )

    def straight_copy(c):
        return pltpu.make_async_remote_copy(
            src_ref=slot(c, straight - width, None),
            dst_ref=slot(c, straight, None),
            send_sem=straight_sem.at[0],
            recv_sem=arrival(c, straight, None),
            device_id=(section, me + width),
            device_id_type=MESH,
        )

    def row_copy(c, index, p):
        k, dx = row_moves[index]
        return pltpu.make_async_remote_copy(
            src_ref=slot(c, k * width, p),
            dst_ref=slot(c, k * width + dx, p),
            send_sem=row_sem.at[index],
            recv_sem=arrival(c, k * width + dx, p),
            device_id=(section, me + dx),
            device_id_type=MESH,
        )

    def out_copy(c, part):
        first = pl.multiple_of((c % groups) * out_cols + part * part_cols, part_cols)
        return pltpu.make_async_remote_copy(
            src_ref=obuf.at[c, part],
            dst_ref=out_hbm.at[0, c // groups, :, pl.ds(first, part_cols)],
            send_sem=osend_sem,
            recv_sem=orecv_sem,
            device_id=((section + 1) % sections, me),
            device_id_type=MESH,
        )

    def by_piece(c, d, act):
        if d <= (hops - 1) * width:
            act(None)
            return

        @pl.when(c < last)
        def _():
            act(None)

        @pl.when(c == last)
        def _():
            for p in range(halves):
                act(p)

    def column_goes(k):
        return (z + 1 < depth) & (z >= k)

    def row_goes(index):
        k, dx = row_moves[index]
        return (x + dx >= 0) & (x + dx < width) & (z >= k)

    def each_send(k, act):
        if k < hops and (k + 1) * width <= reach:

            @pl.when(column_goes(k))
            def _():
                act(column_copy, k, (k + 1) * width)

        for index, (move_k, dx) in enumerate(row_moves):
            if move_k == k:

                @pl.when(row_goes(index))
                def _(index=index, dx=dx):
                    act(row_copy, index, k * width + dx)

    def start_sends(c, k, p=None):
        def whole(copy, i, d):
            if copy is row_copy and i == eased:

                @pl.when(jnp.logical_not(goes_straight(c)))
                def _():
                    by_piece(c, d, lambda q: copy(c, i, q).start())

            else:
                by_piece(c, d, lambda q: copy(c, i, q).start())

        if p is None:
            each_send(k, whole)
        else:
            each_send(k, lambda copy, i, d: copy(c, i, p).start())

    def arrived(c, d, p):
        @pl.when(me >= d)
        def _():
            pltpu.make_async_copy(slot(c, d, p), slot(c, d, p), arrival(c, d, p)).wait()

    def arrived_and_on(c, k):
        def act(p):
            arrived(c, k * width, p)
            start_sends(c, k, p)

        by_piece(c, k * width, act)

    barrier = pltpu.get_barrier_semaphore()

    def greet(condition, target):
        @pl.when(condition)
        def _():
            pl.semaphore_signal(barrier, inc=1, device_id=target, device_id_type=MESH)

    greet(z > 0, (section, me - width))
    greet(z + 1 < depth, (section, me + width))
    for dx in range(1 - width, width):
        if dx != 0:
            greet((x + dx >= 0) & (x + dx < width), (section, me + dx))
    for step in (1, sections - 1):
        greet(me >= 0, ((section + step) % sections, me))

    kv_copies = [
        pltpu.make_async_copy(kv_hbm.at[0, m], raw.at[m], local_sem.at[1 + m]) for m in range(micro)
    ]
    q_copy = pltpu.make_async_copy(q_hbm.at[0], qbuf, local_sem.at[0])
    for copy in kv_copies:
        copy.start()
    q_copy.start()
    for copy in kv_copies:
        copy.wait()

    def by_head(j, then):
        for half in range(2):
            one = raw[order_ref[0, j], :, :, pl.ds(half * head, head)]
            spread[half] = one.astype(jnp.float32).reshape(tok * groups, head)
        for g in range(groups):
            for half in range(2):
                kvbuf[j * groups + g, pl.ds(0, tok), pl.ds(half * head, head)] = spread[
                    half, pl.ds(g, tok, stride=groups), :
                ].astype(kvbuf.dtype)
            then(g)

    leads = [min(LEAD, groups), min(2, groups), 1]
    turns = [0, chunks // 2, chunks * 3 // 4, chunks]

    def first_sends(g):
        if g == 0:
            column_mates = jnp.where(z > 0, 1, 0) + jnp.where(z + 1 < depth, 1, 0)
            pl.semaphore_wait(barrier, column_mates + (width - 1) + 2)
        if g < leads[0]:
            start_sends(jnp.int32(g), 0)

    by_head(0, first_sends)
    for j in range(1, micro):
        by_head(j, lambda g: None)

    for d in range(1, reach + 1):

        @pl.when(me < d)
        def _(d=d):
            def clear(c, carry):
                kvbuf[c, pl.ds(d * tok, tok), :] = jnp.zeros((tok, pair), kvbuf.dtype)
                return carry

            lax.fori_loop(0, chunks, clear, 0)

    for j in range(micro):
        m = order_ref[0, j]
        own = me * tok + lax.broadcasted_iota(jnp.int32, (tok, tok), 0)
        end = jnp.int32(0)
        begin = jnp.zeros((tok, tok), jnp.int32)
        for document in range(docs):
            end = end + lengths_ref[0, m, document]
            begin = jnp.where(own >= end, end, begin)
        for d in range(reach + 1):
            other = (me - d) * tok + lax.broadcasted_iota(jnp.int32, (tok, tok), 1)
            allowed = (other >= begin) & (other <= own)
            bias[j, :, pl.ds(d * tok, tok)] = jnp.where(allowed, 0.0, MASKED)

    q_copy.wait()
    factor = head**-0.5 * math.log2(math.e)

    def compute(c, turn_parts):
        j = c // groups
        k = kvbuf[c, :, :head]
        v = jnp.concatenate([kvbuf[c, :, head:], jnp.ones((keys, head), kvbuf.dtype)], axis=1)
        for part in turn_parts:
            first = pl.multiple_of((c % groups) * out_cols + part * part_cols, part_cols)
            q = qbuf[order_ref[0, j], :, pl.ds(first, part_cols)]
            stacked = jnp.concatenate(
                [q[:, i * head : (i + 1) * head] for i in range(joint)], axis=0
            )
            scores = lax.dot_general(
                stacked, k, (((1,), (1,)), ((), ())), preferred_element_type=jnp.float32
            )
            weights = []
            for top in range(0, joint * tok, block):
                hidden = bias[j, pl.ds(top % tok, block), :]
                logits = scores[top : top + block] * factor + hidden
                lifted = logits - jnp.max(logits, axis=1, keepdims=True)
                weights.append(jnp.exp2(lifted).astype(jnp.bfloat16))
            mixed = jnp.dot(
                jnp.concatenate(weights, axis=0), v, preferred_element_type=jnp.float32
            )
            result = (mixed[:, :head] / mixed[:, head:]).astype(obuf.dtype)
            for i in range(joint):
                obuf[c, part, :, i * head : (i + 1) * head] = result[i * tok : (i + 1) * tok]
            out_copy(c, part).start()

    def turn(t, carry):
        for lead, begin, end in zip(leads, turns, turns[1:]):
            begin = max(begin, leads[0])

            @pl.when((t + lead >= begin) & (t + lead < end))
            def _(lead=lead):
                start_sends(t + lead, 0)

        for k in range(1, hops + 1):
            if k * width <= reach:

                @pl.when((t - (k - 1) >= 0) & (t - (k - 1) < chunks))
                def _(k=k):
                    arrived_and_on(t - (k - 1), k)

            @pl.when(t >= hops)
            def _(k=k):
                c = t - hops
                if k == 1:
                    for d in range(1, reach + 1):
                        if d % width != 0:
                            by_piece(c, d, lambda p, d=d: arrived(c, d, p))
                    if eased is not None:

                        @pl.when(goes_straight(c) & straight_goes())
                        def _():
                            straight_copy(c).start()

                compute(c, range((k - 1) * parts // hops, k * parts // hops))

        return carry

    lax.fori_loop(0, chunks + hops, turn, 0)

    def sent(ref, sem):
        pltpu.make_async_copy(ref, ref, sem).wait()

    def drained(k, count=chunks):
        return kvbuf.at[pl.ds(0, count), pl.ds(k * width * tok, tok), :]

    for k in range(hops):
        if (k + 1) * width <= reach:

            @pl.when(column_goes(k))
            def _(k=k):
                sent(drained(k), column_sem.at[k])

    for index, (k, _) in enumerate(row_moves):

        @pl.when(row_goes(index))
        def _(k=k, index=index):
            sent(drained(k, chunks - straight_count * (index == eased)), row_sem.at[index])

    if eased is not None:

        @pl.when(straight_goes())
        def _():
            sent(drained(0, straight_count), straight_sem.at[0])

    sent(obuf, osend_sem)
    sent(out_hbm.at[0], orecv_sem)


def local(queries, keys_values, lengths, order):
    n = lax.axis_size("seq")
    width = row_width(n)
    reach = n // 2
    hops = -(-reach // width)
    _, micro, tok, q_cols = queries.shape
    groups, pair = keys_values.shape[3:]
    chunks = micro * groups
    out_cols = q_cols // groups
    moves = sum(
        1
        for k in range(hops + 1)
        for dx in range(1 - width, width)
        if dx != 0 and 1 <= k * width + dx <= reach
    )

    head = pair // 2
    share = out_cols // head
    joint = 2 if share % 2 == 0 else 1
    keys = (reach + 1) * tok
    inputs = [
        pltpu.with_memory_space_constraint(a, pltpu.HBM)
        for a in (lengths, order, queries, keys_values)
    ]
    return pl.pallas_call(
        kernel,
        out_shape=jax.ShapeDtypeStruct(queries.shape, queries.dtype),
        in_specs=[
            pl.BlockSpec(memory_space=pltpu.SMEM),
            pl.BlockSpec(memory_space=pltpu.SMEM),
            pl.BlockSpec(memory_space=pltpu.HBM),
            pl.BlockSpec(memory_space=pltpu.HBM),
        ],
        out_specs=pl.BlockSpec(memory_space=pl.ANY),
        scratch_shapes=[
            pltpu.VMEM((micro, tok, groups, pair), jnp.bfloat16),
            pltpu.VMEM((2, tok * groups, pair // 2), jnp.float32),
            pltpu.VMEM((chunks, keys, pair), jnp.bfloat16),
            pltpu.VMEM((micro, tok, q_cols), jnp.bfloat16),
            pltpu.VMEM((chunks, share // joint, tok, joint * head), jnp.bfloat16),
            pltpu.VMEM((micro, tok, keys), jnp.float32),
            pltpu.SemaphoreType.DMA((1 + micro,)),
            pltpu.SemaphoreType.DMA((reach + 1, chunks + 1)),
            pltpu.SemaphoreType.DMA((hops,)),
            pltpu.SemaphoreType.DMA((max(1, moves),)),
            pltpu.SemaphoreType.DMA((1,)),
            pltpu.SemaphoreType.DMA(()),
            pltpu.SemaphoreType.DMA(()),
        ],
        compiler_params=pltpu.CompilerParams(
            collective_id=0,
            has_side_effects=True,
            vmem_limit_bytes=40 * 1024 * 1024,
        ),
        name="relay_attention",
    )(*inputs)


def solution(mesh):
    placed = (
        P("section", None, "seq", None),
        P("section", None, "seq", None, None),
        P("section", None, None),
        P("section", None),
    )
    return jax.shard_map(
        local,
        mesh=mesh,
        in_specs=placed,
        out_specs=P("section", None, "seq", None),
        check_vma=False,
    )
```

```python
import math

import jax
import jax.numpy as jnp
from jax import lax
from jax.experimental import pallas as pl
from jax.experimental.pallas import tpu as pltpu
from jax.sharding import PartitionSpec as P

MESH = pl.DeviceIdType.MESH
LEAD = 3
LAG = 1
MASKED = -1e30


def row_width(count):
    return max(w for w in range(1, count + 1) if count % w == 0 and w * w <= count)


def kernel(
    lengths_ref,
    order_ref,
    q_hbm,
    kv_hbm,
    out_hbm,
    raw,
    spread,
    kvbuf,
    qbuf,
    obuf,
    bias,
    local_sem,
    recv_sem,
    column_sem,
    row_sem,
    osend_sem,
    orecv_sem,
):
    n = lax.axis_size("seq")
    sections = lax.axis_size("section")
    width = row_width(n)
    depth = n // width
    reach = n // 2
    hops = -(-reach // width)
    micro, tok, q_cols = qbuf.shape
    chunks, keys, pair = kvbuf.shape
    head = pair // 2
    groups = chunks // micro
    out_cols = q_cols // groups
    share = out_cols // head
    parts, part_cols = obuf.shape[1], obuf.shape[3]
    joint = part_cols // head
    block = tok // 2
    docs = lengths_ref.shape[2]
    last = chunks - 1
    halves = 2 if tok % 32 == 0 else 1

    me = lax.axis_index("seq")
    section = lax.axis_index("section")
    x = me % width
    z = me // width
    row_moves = [
        (k, dx)
        for k in range(hops + 1)
        for dx in range(1 - width, width)
        if dx != 0 and 1 <= k * width + dx <= reach
    ]

    def slot(c, d, p):
        rows = tok if p is None else tok // halves
        return kvbuf.at[c, pl.ds(d * tok + (p or 0) * rows, rows), :]

    def arrival(c, d, p):
        return recv_sem.at[d, chunks if p == 1 else c]

    def column_copy(c, k, p):
        return pltpu.make_async_remote_copy(
            src_ref=slot(c, k * width, p),
            dst_ref=slot(c, (k + 1) * width, p),
            send_sem=column_sem.at[k],
            recv_sem=arrival(c, (k + 1) * width, p),
            device_id=(section, me + width),
            device_id_type=MESH,
        )

    def row_copy(c, index, p):
        k, dx = row_moves[index]
        return pltpu.make_async_remote_copy(
            src_ref=slot(c, k * width, p),
            dst_ref=slot(c, k * width + dx, p),
            send_sem=row_sem.at[index],
            recv_sem=arrival(c, k * width + dx, p),
            device_id=(section, me + dx),
            device_id_type=MESH,
        )

    def out_copy(c, part):
        first = pl.multiple_of((c % groups) * out_cols + part * part_cols, part_cols)
        return pltpu.make_async_remote_copy(
            src_ref=obuf.at[c, part],
            dst_ref=out_hbm.at[0, c // groups, :, pl.ds(first, part_cols)],
            send_sem=osend_sem,
            recv_sem=orecv_sem,
            device_id=((section + 1) % sections, me),
            device_id_type=MESH,
        )

    def by_piece(c, d, act):
        if d <= (hops - 1) * width:
            act(None)
            return

        @pl.when(c < last)
        def _():
            act(None)

        @pl.when(c == last)
        def _():
            for p in range(halves):
                act(p)

    def column_goes(k):
        return (z + 1 < depth) & (z >= k)

    def row_goes(index):
        k, dx = row_moves[index]
        return (x + dx >= 0) & (x + dx < width) & (z >= k)

    def each_send(k, act):
        if k < hops and (k + 1) * width <= reach:

            @pl.when(column_goes(k))
            def _():
                act(column_copy, k, (k + 1) * width)

        for index, (move_k, dx) in enumerate(row_moves):
            if move_k == k:

                @pl.when(row_goes(index))
                def _(index=index, dx=dx):
                    act(row_copy, index, k * width + dx)

    def start_sends(c, k, p=None):
        if p is None:
            each_send(k, lambda copy, i, d: by_piece(c, d, lambda q: copy(c, i, q).start()))
        else:
            each_send(k, lambda copy, i, d: copy(c, i, p).start())

    def arrived(c, d, p):
        @pl.when(me >= d)
        def _():
            pltpu.make_async_copy(slot(c, d, p), slot(c, d, p), arrival(c, d, p)).wait()

    def arrived_and_on(c, k):
        def act(p):
            arrived(c, k * width, p)
            start_sends(c, k, p)

        by_piece(c, k * width, act)

    barrier = pltpu.get_barrier_semaphore()

    def greet(condition, target):
        @pl.when(condition)
        def _():
            pl.semaphore_signal(barrier, inc=1, device_id=target, device_id_type=MESH)

    greet(z > 0, (section, me - width))
    greet(z + 1 < depth, (section, me + width))
    for dx in range(1 - width, width):
        if dx != 0:
            greet((x + dx >= 0) & (x + dx < width), (section, me + dx))
    for step in (1, sections - 1):
        greet(me >= 0, ((section + step) % sections, me))

    kv_copies = [
        pltpu.make_async_copy(kv_hbm.at[0, m], raw.at[m], local_sem.at[1 + m]) for m in range(micro)
    ]
    q_copy = pltpu.make_async_copy(q_hbm.at[0], qbuf, local_sem.at[0])
    for copy in kv_copies:
        copy.start()
    q_copy.start()
    for copy in kv_copies:
        copy.wait()

    def by_head(j, then):
        for half in range(2):
            one = raw[order_ref[0, j], :, :, pl.ds(half * head, head)]
            spread[half] = one.astype(jnp.float32).reshape(tok * groups, head)
        for g in range(groups):
            for half in range(2):
                kvbuf[j * groups + g, pl.ds(0, tok), pl.ds(half * head, head)] = spread[
                    half, pl.ds(g, tok, stride=groups), :
                ].astype(kvbuf.dtype)
            then(g)

    leads = [min(LEAD, groups), min(2, groups), 1]
    turns = [0, chunks // 2, chunks * 3 // 4, chunks]

    def first_sends(g):
        if g == 0:
            column_mates = jnp.where(z > 0, 1, 0) + jnp.where(z + 1 < depth, 1, 0)
            pl.semaphore_wait(barrier, column_mates + (width - 1) + 2)
        if g < leads[0]:
            start_sends(jnp.int32(g), 0)

    by_head(0, first_sends)
    for j in range(1, micro):
        by_head(j, lambda g: None)

    for d in range(1, reach + 1):

        @pl.when(me < d)
        def _(d=d):
            def clear(c, carry):
                kvbuf[c, pl.ds(d * tok, tok), :] = jnp.zeros((tok, pair), kvbuf.dtype)
                return carry

            lax.fori_loop(0, chunks, clear, 0)

    for j in range(micro):
        m = order_ref[0, j]
        own = me * tok + lax.broadcasted_iota(jnp.int32, (tok, tok), 0)
        end = jnp.int32(0)
        begin = jnp.zeros((tok, tok), jnp.int32)
        for document in range(docs):
            end = end + lengths_ref[0, m, document]
            begin = jnp.where(own >= end, end, begin)
        for d in range(reach + 1):
            other = (me - d) * tok + lax.broadcasted_iota(jnp.int32, (tok, tok), 1)
            allowed = (other >= begin) & (other <= own)
            bias[j, :, pl.ds(d * tok, tok)] = jnp.where(allowed, 0.0, MASKED)

    q_copy.wait()
    factor = head**-0.5 * math.log2(math.e)

    def compute(c, turn_parts):
        j = c // groups
        k = kvbuf[c, :, :head]
        v = jnp.concatenate([kvbuf[c, :, head:], jnp.ones((keys, head), kvbuf.dtype)], axis=1)
        for part in turn_parts:
            first = pl.multiple_of((c % groups) * out_cols + part * part_cols, part_cols)
            q = qbuf[order_ref[0, j], :, pl.ds(first, part_cols)]
            stacked = jnp.concatenate(
                [q[:, i * head : (i + 1) * head] for i in range(joint)], axis=0
            )
            scores = lax.dot_general(
                stacked, k, (((1,), (1,)), ((), ())), preferred_element_type=jnp.float32
            )
            weights = []
            for top in range(0, joint * tok, block):
                hidden = bias[j, pl.ds(top % tok, block), :]
                logits = scores[top : top + block] * factor + hidden
                lifted = logits - jnp.max(logits, axis=1, keepdims=True)
                weights.append(jnp.exp2(lifted).astype(jnp.bfloat16))
            mixed = jnp.dot(
                jnp.concatenate(weights, axis=0), v, preferred_element_type=jnp.float32
            )
            result = (mixed[:, :head] / mixed[:, head:]).astype(obuf.dtype)
            for i in range(joint):
                obuf[c, part, :, i * head : (i + 1) * head] = result[i * tok : (i + 1) * tok]
            out_copy(c, part).start()

    def turn(t, carry):
        for lead, begin, end in zip(leads, turns, turns[1:]):
            begin = max(begin, leads[0])

            @pl.when((t + lead >= begin) & (t + lead < end))
            def _(lead=lead):
                start_sends(t + lead, 0)

        for k in range(1, hops + 1):
            if k * width <= reach:

                @pl.when((t - (k - 1) >= 0) & (t - (k - 1) < chunks))
                def _(k=k):
                    arrived_and_on(t - (k - 1), k)

            @pl.when(t >= hops + LAG)
            def _(k=k):
                c = t - hops - LAG
                if k == 1:
                    for d in range(1, reach + 1):
                        if d % width != 0:
                            by_piece(c, d, lambda p, d=d: arrived(c, d, p))
                compute(c, range((k - 1) * parts // hops, k * parts // hops))

        return carry

    lax.fori_loop(0, chunks + hops + LAG, turn, 0)

    def sent(ref, sem):
        pltpu.make_async_copy(ref, ref, sem).wait()

    def drained(k):
        return kvbuf.at[:, pl.ds(k * width * tok, tok), :]

    for k in range(hops):
        if (k + 1) * width <= reach:

            @pl.when(column_goes(k))
            def _(k=k):
                sent(drained(k), column_sem.at[k])

    for index, (k, _) in enumerate(row_moves):

        @pl.when(row_goes(index))
        def _(k=k, index=index):
            sent(drained(k), row_sem.at[index])

    sent(obuf, osend_sem)
    sent(out_hbm.at[0], orecv_sem)


def local(queries, keys_values, lengths, order):
    n = lax.axis_size("seq")
    width = row_width(n)
    reach = n // 2
    hops = -(-reach // width)
    _, micro, tok, q_cols = queries.shape
    groups, pair = keys_values.shape[3:]
    chunks = micro * groups
    out_cols = q_cols // groups
    moves = sum(
        1
        for k in range(hops + 1)
        for dx in range(1 - width, width)
        if dx != 0 and 1 <= k * width + dx <= reach
    )

    head = pair // 2
    share = out_cols // head
    joint = 2 if share % 2 == 0 else 1
    keys = (reach + 1) * tok
    inputs = [
        pltpu.with_memory_space_constraint(a, pltpu.HBM)
        for a in (lengths, order, queries, keys_values)
    ]
    return pl.pallas_call(
        kernel,
        out_shape=jax.ShapeDtypeStruct(queries.shape, queries.dtype),
        in_specs=[
            pl.BlockSpec(memory_space=pltpu.SMEM),
            pl.BlockSpec(memory_space=pltpu.SMEM),
            pl.BlockSpec(memory_space=pltpu.HBM),
            pl.BlockSpec(memory_space=pltpu.HBM),
        ],
        out_specs=pl.BlockSpec(memory_space=pl.ANY),
        scratch_shapes=[
            pltpu.VMEM((micro, tok, groups, pair), jnp.bfloat16),
            pltpu.VMEM((2, tok * groups, pair // 2), jnp.float32),
            pltpu.VMEM((chunks, keys, pair), jnp.bfloat16),
            pltpu.VMEM((micro, tok, q_cols), jnp.bfloat16),
            pltpu.VMEM((chunks, share // joint, tok, joint * head), jnp.bfloat16),
            pltpu.VMEM((micro, tok, keys), jnp.float32),
            pltpu.SemaphoreType.DMA((1 + micro,)),
            pltpu.SemaphoreType.DMA((reach + 1, chunks + 1)),
            pltpu.SemaphoreType.DMA((hops,)),
            pltpu.SemaphoreType.DMA((max(1, moves),)),
            pltpu.SemaphoreType.DMA(()),
            pltpu.SemaphoreType.DMA(()),
        ],
        compiler_params=pltpu.CompilerParams(
            collective_id=0,
            has_side_effects=True,
            vmem_limit_bytes=40 * 1024 * 1024,
        ),
        name="relay_attention",
    )(*inputs)


def solution(mesh):
    placed = (
        P("section", None, "seq", None),
        P("section", None, "seq", None, None),
        P("section", None, None),
        P("section", None),
    )
    return jax.shard_map(
        local,
        mesh=mesh,
        in_specs=placed,
        out_specs=P("section", None, "seq", None),
        check_vma=False,
    )
```

```python
import math

import jax
import jax.numpy as jnp
from jax import lax
from jax.experimental import pallas as pl
from jax.experimental.pallas import tpu as pltpu
from jax.sharding import PartitionSpec as P

MESH = pl.DeviceIdType.MESH
LEAD = 1
LAG = 1
MASKED = -1e30


def row_width(count):
    return max(w for w in range(1, count + 1) if count % w == 0 and w * w <= count)


def kernel(
    lengths_ref,
    order_ref,
    q_hbm,
    kv_hbm,
    out_hbm,
    raw,
    spread,
    kvbuf,
    qbuf,
    obuf,
    bias,
    local_sem,
    recv_sem,
    column_sem,
    row_sem,
    osend_sem,
    orecv_sem,
):
    n = lax.axis_size("seq")
    sections = lax.axis_size("section")
    width = row_width(n)
    depth = n // width
    reach = n // 2
    hops = -(-reach // width)
    micro, tok, q_cols = qbuf.shape
    chunks, keys, pair = kvbuf.shape
    head = pair // 2
    groups = chunks // micro
    out_cols = q_cols // groups
    share = out_cols // head
    parts, part_cols = obuf.shape[1], obuf.shape[3]
    joint = part_cols // head
    block = tok // 2
    docs = lengths_ref.shape[2]
    last = chunks - 1
    halves = 2 if tok % 32 == 0 else 1

    me = lax.axis_index("seq")
    section = lax.axis_index("section")
    x = me % width
    z = me // width
    row_moves = [
        (k, dx)
        for k in range(hops + 1)
        for dx in range(1 - width, width)
        if dx != 0 and 1 <= k * width + dx <= reach
    ]

    def slot(c, d, p):
        rows = tok if p is None else tok // halves
        return kvbuf.at[c, pl.ds(d * tok + (p or 0) * rows, rows), :]

    def arrival(c, d, p):
        return recv_sem.at[d, chunks if p == 1 else c]

    def column_copy(c, k, p):
        return pltpu.make_async_remote_copy(
            src_ref=slot(c, k * width, p),
            dst_ref=slot(c, (k + 1) * width, p),
            send_sem=column_sem.at[k],
            recv_sem=arrival(c, (k + 1) * width, p),
            device_id=(section, me + width),
            device_id_type=MESH,
        )

    def row_copy(c, index, p):
        k, dx = row_moves[index]
        return pltpu.make_async_remote_copy(
            src_ref=slot(c, k * width, p),
            dst_ref=slot(c, k * width + dx, p),
            send_sem=row_sem.at[index],
            recv_sem=arrival(c, k * width + dx, p),
            device_id=(section, me + dx),
            device_id_type=MESH,
        )

    def out_copy(c, part):
        first = pl.multiple_of((c % groups) * out_cols + part * part_cols, part_cols)
        return pltpu.make_async_remote_copy(
            src_ref=obuf.at[c, part],
            dst_ref=out_hbm.at[0, c // groups, :, pl.ds(first, part_cols)],
            send_sem=osend_sem,
            recv_sem=orecv_sem,
            device_id=((section + 1) % sections, me),
            device_id_type=MESH,
        )

    def by_piece(c, d, act):
        if d <= (hops - 1) * width:
            act(None)
            return

        @pl.when(c < last)
        def _():
            act(None)

        @pl.when(c == last)
        def _():
            for p in range(halves):
                act(p)

    def column_goes(k):
        return (z + 1 < depth) & (z >= k)

    def row_goes(index):
        k, dx = row_moves[index]
        return (x + dx >= 0) & (x + dx < width) & (z >= k)

    def each_send(k, act):
        if k < hops and (k + 1) * width <= reach:

            @pl.when(column_goes(k))
            def _():
                act(column_copy, k, (k + 1) * width)

        for index, (move_k, dx) in enumerate(row_moves):
            if move_k == k:

                @pl.when(row_goes(index))
                def _(index=index, dx=dx):
                    act(row_copy, index, k * width + dx)

    def start_sends(c, k, p=None):
        if p is None:
            each_send(k, lambda copy, i, d: by_piece(c, d, lambda q: copy(c, i, q).start()))
        else:
            each_send(k, lambda copy, i, d: copy(c, i, p).start())

    def arrived(c, d, p):
        @pl.when(me >= d)
        def _():
            pltpu.make_async_copy(slot(c, d, p), slot(c, d, p), arrival(c, d, p)).wait()

    def arrived_and_on(c, k):
        def act(p):
            arrived(c, k * width, p)
            start_sends(c, k, p)

        by_piece(c, k * width, act)

    barrier = pltpu.get_barrier_semaphore()

    def greet(condition, target):
        @pl.when(condition)
        def _():
            pl.semaphore_signal(barrier, inc=1, device_id=target, device_id_type=MESH)

    greet(z > 0, (section, me - width))
    greet(z + 1 < depth, (section, me + width))
    for dx in range(1 - width, width):
        if dx != 0:
            greet((x + dx >= 0) & (x + dx < width), (section, me + dx))
    for step in (1, sections - 1):
        greet(me >= 0, ((section + step) % sections, me))

    kv_copies = [
        pltpu.make_async_copy(kv_hbm.at[0, m], raw.at[m], local_sem.at[1 + m]) for m in range(micro)
    ]
    q_copy = pltpu.make_async_copy(q_hbm.at[0], qbuf, local_sem.at[0])
    for copy in kv_copies:
        copy.start()
    q_copy.start()
    for copy in kv_copies:
        copy.wait()

    def by_head(j, then):
        for half in range(2):
            one = raw[order_ref[0, j], :, :, pl.ds(half * head, head)]
            spread[half] = one.astype(jnp.float32).reshape(tok * groups, head)
        for g in range(groups):
            for half in range(2):
                kvbuf[j * groups + g, pl.ds(0, tok), pl.ds(half * head, head)] = spread[
                    half, pl.ds(g, tok, stride=groups), :
                ].astype(kvbuf.dtype)
            then(g)

    leads = [min(LEAD, groups), min(2, LEAD), 1]
    turns = [0, chunks // 2, chunks * 3 // 4, chunks]

    def first_sends(g):
        if g == 0:
            column_mates = jnp.where(z > 0, 1, 0) + jnp.where(z + 1 < depth, 1, 0)
            pl.semaphore_wait(barrier, column_mates + (width - 1) + 2)
        if g < leads[0]:
            start_sends(jnp.int32(g), 0)

    by_head(0, first_sends)
    for j in range(1, micro):
        by_head(j, lambda g: None)

    for d in range(1, reach + 1):

        @pl.when(me < d)
        def _(d=d):
            def clear(c, carry):
                kvbuf[c, pl.ds(d * tok, tok), :] = jnp.zeros((tok, pair), kvbuf.dtype)
                return carry

            lax.fori_loop(0, chunks, clear, 0)

    for j in range(micro):
        m = order_ref[0, j]
        own = me * tok + lax.broadcasted_iota(jnp.int32, (tok, tok), 0)
        end = jnp.int32(0)
        begin = jnp.zeros((tok, tok), jnp.int32)
        for document in range(docs):
            end = end + lengths_ref[0, m, document]
            begin = jnp.where(own >= end, end, begin)
        for d in range(reach + 1):
            other = (me - d) * tok + lax.broadcasted_iota(jnp.int32, (tok, tok), 1)
            allowed = (other >= begin) & (other <= own)
            bias[j, :, pl.ds(d * tok, tok)] = jnp.where(allowed, 0.0, MASKED)

    q_copy.wait()
    factor = head**-0.5 * math.log2(math.e)

    def compute(c, turn_parts):
        j = c // groups
        k = kvbuf[c, :, :head]
        v = jnp.concatenate([kvbuf[c, :, head:], jnp.ones((keys, head), kvbuf.dtype)], axis=1)
        for part in turn_parts:
            first = pl.multiple_of((c % groups) * out_cols + part * part_cols, part_cols)
            q = qbuf[order_ref[0, j], :, pl.ds(first, part_cols)]
            stacked = jnp.concatenate(
                [q[:, i * head : (i + 1) * head] for i in range(joint)], axis=0
            )
            scores = lax.dot_general(
                stacked, k, (((1,), (1,)), ((), ())), preferred_element_type=jnp.float32
            )
            weights = []
            for top in range(0, joint * tok, block):
                hidden = bias[j, pl.ds(top % tok, block), :]
                logits = scores[top : top + block] * factor + hidden
                lifted = logits - jnp.max(logits, axis=1, keepdims=True)
                weights.append(jnp.exp2(lifted).astype(jnp.bfloat16))
            mixed = jnp.dot(
                jnp.concatenate(weights, axis=0), v, preferred_element_type=jnp.float32
            )
            result = (mixed[:, :head] / mixed[:, head:]).astype(obuf.dtype)
            for i in range(joint):
                obuf[c, part, :, i * head : (i + 1) * head] = result[i * tok : (i + 1) * tok]
            out_copy(c, part).start()

    def turn(t, carry):
        for lead, begin, end in zip(leads, turns, turns[1:]):
            begin = max(begin, leads[0])

            @pl.when((t + lead >= begin) & (t + lead < end))
            def _(lead=lead):
                start_sends(t + lead, 0)

        for k in range(1, hops + 1):
            if k * width <= reach:

                @pl.when((t - (k - 1) >= 0) & (t - (k - 1) < chunks))
                def _(k=k):
                    arrived_and_on(t - (k - 1), k)

            @pl.when(t >= hops + LAG)
            def _(k=k):
                c = t - hops - LAG
                if k == 1:
                    for d in range(1, reach + 1):
                        if d % width != 0:
                            by_piece(c, d, lambda p, d=d: arrived(c, d, p))
                compute(c, range((k - 1) * parts // hops, k * parts // hops))

        return carry

    lax.fori_loop(0, chunks + hops + LAG, turn, 0)

    def sent(ref, sem):
        pltpu.make_async_copy(ref, ref, sem).wait()

    def drained(k):
        return kvbuf.at[:, pl.ds(k * width * tok, tok), :]

    for k in range(hops):
        if (k + 1) * width <= reach:

            @pl.when(column_goes(k))
            def _(k=k):
                sent(drained(k), column_sem.at[k])

    for index, (k, _) in enumerate(row_moves):

        @pl.when(row_goes(index))
        def _(k=k, index=index):
            sent(drained(k), row_sem.at[index])

    sent(obuf, osend_sem)
    sent(out_hbm.at[0], orecv_sem)


def local(queries, keys_values, lengths, order):
    n = lax.axis_size("seq")
    width = row_width(n)
    reach = n // 2
    hops = -(-reach // width)
    _, micro, tok, q_cols = queries.shape
    groups, pair = keys_values.shape[3:]
    chunks = micro * groups
    out_cols = q_cols // groups
    moves = sum(
        1
        for k in range(hops + 1)
        for dx in range(1 - width, width)
        if dx != 0 and 1 <= k * width + dx <= reach
    )

    head = pair // 2
    share = out_cols // head
    joint = 2 if share % 2 == 0 else 1
    keys = (reach + 1) * tok
    inputs = [
        pltpu.with_memory_space_constraint(a, pltpu.HBM)
        for a in (lengths, order, queries, keys_values)
    ]
    return pl.pallas_call(
        kernel,
        out_shape=jax.ShapeDtypeStruct(queries.shape, queries.dtype),
        in_specs=[
            pl.BlockSpec(memory_space=pltpu.SMEM),
            pl.BlockSpec(memory_space=pltpu.SMEM),
            pl.BlockSpec(memory_space=pltpu.HBM),
            pl.BlockSpec(memory_space=pltpu.HBM),
        ],
        out_specs=pl.BlockSpec(memory_space=pl.ANY),
        scratch_shapes=[
            pltpu.VMEM((micro, tok, groups, pair), jnp.bfloat16),
            pltpu.VMEM((2, tok * groups, pair // 2), jnp.float32),
            pltpu.VMEM((chunks, keys, pair), jnp.bfloat16),
            pltpu.VMEM((micro, tok, q_cols), jnp.bfloat16),
            pltpu.VMEM((chunks, share // joint, tok, joint * head), jnp.bfloat16),
            pltpu.VMEM((micro, tok, keys), jnp.float32),
            pltpu.SemaphoreType.DMA((1 + micro,)),
            pltpu.SemaphoreType.DMA((reach + 1, chunks + 1)),
            pltpu.SemaphoreType.DMA((hops,)),
            pltpu.SemaphoreType.DMA((max(1, moves),)),
            pltpu.SemaphoreType.DMA(()),
            pltpu.SemaphoreType.DMA(()),
        ],
        compiler_params=pltpu.CompilerParams(
            collective_id=0,
            has_side_effects=True,
            vmem_limit_bytes=40 * 1024 * 1024,
        ),
        name="relay_attention",
    )(*inputs)


def solution(mesh):
    placed = (
        P("section", None, "seq", None),
        P("section", None, "seq", None, None),
        P("section", None, None),
        P("section", None),
    )
    return jax.shard_map(
        local,
        mesh=mesh,
        in_specs=placed,
        out_specs=P("section", None, "seq", None),
        check_vma=False,
    )
```

```python
import math

import jax
import jax.numpy as jnp
from jax import lax
from jax.experimental import pallas as pl
from jax.experimental.pallas import tpu as pltpu
from jax.sharding import PartitionSpec as P

MESH = pl.DeviceIdType.MESH
LEAD = 1
LAG = 1
MASKED = -1e30


def row_width(count):
    return max(w for w in range(1, count + 1) if count % w == 0 and w * w <= count)


def kernel(
    lengths_ref,
    order_ref,
    q_hbm,
    kv_hbm,
    out_hbm,
    raw,
    spread,
    kvbuf,
    qbuf,
    obuf,
    bias,
    local_sem,
    recv_sem,
    column_sem,
    row_sem,
    osend_sem,
    orecv_sem,
):
    n = lax.axis_size("seq")
    sections = lax.axis_size("section")
    width = row_width(n)
    depth = n // width
    reach = n // 2
    hops = -(-reach // width)
    micro, tok, q_cols = qbuf.shape
    chunks, keys, pair = kvbuf.shape
    head = pair // 2
    groups = chunks // micro
    out_cols = q_cols // groups
    share = out_cols // head
    parts, part_cols = obuf.shape[1], obuf.shape[3]
    joint = part_cols // head
    block = tok // 2
    docs = lengths_ref.shape[2]
    last = chunks - 1
    halves = 2 if tok % 32 == 0 else 1

    me = lax.axis_index("seq")
    section = lax.axis_index("section")
    x = me % width
    z = me // width
    row_moves = [
        (k, dx)
        for k in range(hops + 1)
        for dx in range(1 - width, width)
        if dx != 0 and 1 <= k * width + dx <= reach
    ]

    def slot(c, d, p):
        rows = tok if p is None else tok // halves
        return kvbuf.at[c, pl.ds(d * tok + (p or 0) * rows, rows), :]

    def arrival(c, d, p):
        return recv_sem.at[d, chunks + jnp.where(c == 0, 1, 0) if p == 1 else c]

    def column_copy(c, k, p):
        return pltpu.make_async_remote_copy(
            src_ref=slot(c, k * width, p),
            dst_ref=slot(c, (k + 1) * width, p),
            send_sem=column_sem.at[k],
            recv_sem=arrival(c, (k + 1) * width, p),
            device_id=(section, me + width),
            device_id_type=MESH,
        )

    def row_copy(c, index, p):
        k, dx = row_moves[index]
        return pltpu.make_async_remote_copy(
            src_ref=slot(c, k * width, p),
            dst_ref=slot(c, k * width + dx, p),
            send_sem=row_sem.at[index],
            recv_sem=arrival(c, k * width + dx, p),
            device_id=(section, me + dx),
            device_id_type=MESH,
        )

    def out_copy(c, part):
        first = pl.multiple_of((c % groups) * out_cols + part * part_cols, part_cols)
        return pltpu.make_async_remote_copy(
            src_ref=obuf.at[c, part],
            dst_ref=out_hbm.at[0, c // groups, :, pl.ds(first, part_cols)],
            send_sem=osend_sem,
            recv_sem=orecv_sem,
            device_id=((section + 1) % sections, me),
            device_id_type=MESH,
        )

    def by_piece(c, d, act):
        cut = c == 0
        if d > (hops - 1) * width:
            cut = cut | (c == last)

        @pl.when(jnp.logical_not(cut))
        def _():
            act(None)

        @pl.when(cut)
        def _():
            for p in range(halves):
                act(p)

    def column_goes(k):
        return (z + 1 < depth) & (z >= k)

    def row_goes(index):
        k, dx = row_moves[index]
        return (x + dx >= 0) & (x + dx < width) & (z >= k)

    def each_send(k, act):
        if k < hops and (k + 1) * width <= reach:

            @pl.when(column_goes(k))
            def _():
                act(column_copy, k, (k + 1) * width)

        for index, (move_k, dx) in enumerate(row_moves):
            if move_k == k:

                @pl.when(row_goes(index))
                def _(index=index, dx=dx):
                    act(row_copy, index, k * width + dx)

    def start_sends(c, k, p=None):
        if p is None:
            each_send(k, lambda copy, i, d: by_piece(c, d, lambda q: copy(c, i, q).start()))
        else:
            each_send(k, lambda copy, i, d: copy(c, i, p).start())

    def arrived(c, d, p):
        @pl.when(me >= d)
        def _():
            pltpu.make_async_copy(slot(c, d, p), slot(c, d, p), arrival(c, d, p)).wait()

    def arrived_and_on(c, k):
        def act(p):
            arrived(c, k * width, p)
            start_sends(c, k, p)

        by_piece(c, k * width, act)

    barrier = pltpu.get_barrier_semaphore()

    def greet(condition, target):
        @pl.when(condition)
        def _():
            pl.semaphore_signal(barrier, inc=1, device_id=target, device_id_type=MESH)

    greet(z > 0, (section, me - width))
    greet(z + 1 < depth, (section, me + width))
    for dx in range(1 - width, width):
        if dx != 0:
            greet((x + dx >= 0) & (x + dx < width), (section, me + dx))
    for step in (1, sections - 1):
        greet(me >= 0, ((section + step) % sections, me))

    kv_copies = [
        pltpu.make_async_copy(kv_hbm.at[0, m], raw.at[m], local_sem.at[1 + m]) for m in range(micro)
    ]
    q_copy = pltpu.make_async_copy(q_hbm.at[0], qbuf, local_sem.at[0])
    for copy in kv_copies:
        copy.start()
    q_copy.start()
    for copy in kv_copies:
        copy.wait()

    def by_head(j, then):
        for half in range(2):
            one = raw[order_ref[0, j], :, :, pl.ds(half * head, head)]
            spread[half] = one.astype(jnp.float32).reshape(tok * groups, head)
        for g in range(groups):
            for half in range(2):
                kvbuf[j * groups + g, pl.ds(0, tok), pl.ds(half * head, head)] = spread[
                    half, pl.ds(g, tok, stride=groups), :
                ].astype(kvbuf.dtype)
            then(g)

    leads = [min(LEAD, groups), min(2, LEAD), 1]
    turns = [0, chunks // 2, chunks * 3 // 4, chunks]

    def first_sends(g):
        if g == 0:
            column_mates = jnp.where(z > 0, 1, 0) + jnp.where(z + 1 < depth, 1, 0)
            pl.semaphore_wait(barrier, column_mates + (width - 1) + 2)
        if g < leads[0]:
            start_sends(jnp.int32(g), 0)

    by_head(0, first_sends)
    for j in range(1, micro):
        by_head(j, lambda g: None)

    for d in range(1, reach + 1):

        @pl.when(me < d)
        def _(d=d):
            def clear(c, carry):
                kvbuf[c, pl.ds(d * tok, tok), :] = jnp.zeros((tok, pair), kvbuf.dtype)
                return carry

            lax.fori_loop(0, chunks, clear, 0)

    for j in range(micro):
        m = order_ref[0, j]
        own = me * tok + lax.broadcasted_iota(jnp.int32, (tok, tok), 0)
        end = jnp.int32(0)
        begin = jnp.zeros((tok, tok), jnp.int32)
        for document in range(docs):
            end = end + lengths_ref[0, m, document]
            begin = jnp.where(own >= end, end, begin)
        for d in range(reach + 1):
            other = (me - d) * tok + lax.broadcasted_iota(jnp.int32, (tok, tok), 1)
            allowed = (other >= begin) & (other <= own)
            bias[j, :, pl.ds(d * tok, tok)] = jnp.where(allowed, 0.0, MASKED)

    q_copy.wait()
    factor = head**-0.5 * math.log2(math.e)

    def compute(c, turn_parts):
        j = c // groups
        k = kvbuf[c, :, :head]
        v = jnp.concatenate([kvbuf[c, :, head:], jnp.ones((keys, head), kvbuf.dtype)], axis=1)
        for part in turn_parts:
            first = pl.multiple_of((c % groups) * out_cols + part * part_cols, part_cols)
            q = qbuf[order_ref[0, j], :, pl.ds(first, part_cols)]
            stacked = jnp.concatenate(
                [q[:, i * head : (i + 1) * head] for i in range(joint)], axis=0
            )
            scores = lax.dot_general(
                stacked, k, (((1,), (1,)), ((), ())), preferred_element_type=jnp.float32
            )
            weights = []
            for top in range(0, joint * tok, block):
                hidden = bias[j, pl.ds(top % tok, block), :]
                logits = scores[top : top + block] * factor + hidden
                lifted = logits - jnp.max(logits, axis=1, keepdims=True)
                weights.append(jnp.exp2(lifted).astype(jnp.bfloat16))
            mixed = jnp.dot(
                jnp.concatenate(weights, axis=0), v, preferred_element_type=jnp.float32
            )
            result = (mixed[:, :head] / mixed[:, head:]).astype(obuf.dtype)
            for i in range(joint):
                obuf[c, part, :, i * head : (i + 1) * head] = result[i * tok : (i + 1) * tok]
            out_copy(c, part).start()

    def turn(t, carry):
        for lead, begin, end in zip(leads, turns, turns[1:]):
            begin = max(begin, leads[0])

            @pl.when((t + lead >= begin) & (t + lead < end))
            def _(lead=lead):
                start_sends(t + lead, 0)

        for k in range(1, hops + 1):
            if k * width <= reach:

                @pl.when((t - (k - 1) >= 0) & (t - (k - 1) < chunks))
                def _(k=k):
                    arrived_and_on(t - (k - 1), k)

            @pl.when(t >= hops + LAG)
            def _(k=k):
                c = t - hops - LAG
                if k == 1:
                    for d in range(1, reach + 1):
                        if d % width != 0:
                            by_piece(c, d, lambda p, d=d: arrived(c, d, p))
                compute(c, range((k - 1) * parts // hops, k * parts // hops))

        return carry

    lax.fori_loop(0, chunks + hops + LAG, turn, 0)

    def sent(ref, sem):
        pltpu.make_async_copy(ref, ref, sem).wait()

    def drained(k):
        return kvbuf.at[:, pl.ds(k * width * tok, tok), :]

    for k in range(hops):
        if (k + 1) * width <= reach:

            @pl.when(column_goes(k))
            def _(k=k):
                sent(drained(k), column_sem.at[k])

    for index, (k, _) in enumerate(row_moves):

        @pl.when(row_goes(index))
        def _(k=k, index=index):
            sent(drained(k), row_sem.at[index])

    sent(obuf, osend_sem)
    sent(out_hbm.at[0], orecv_sem)


def local(queries, keys_values, lengths, order):
    n = lax.axis_size("seq")
    width = row_width(n)
    reach = n // 2
    hops = -(-reach // width)
    _, micro, tok, q_cols = queries.shape
    groups, pair = keys_values.shape[3:]
    chunks = micro * groups
    out_cols = q_cols // groups
    moves = sum(
        1
        for k in range(hops + 1)
        for dx in range(1 - width, width)
        if dx != 0 and 1 <= k * width + dx <= reach
    )

    head = pair // 2
    share = out_cols // head
    joint = 2 if share % 2 == 0 else 1
    keys = (reach + 1) * tok
    inputs = [
        pltpu.with_memory_space_constraint(a, pltpu.HBM)
        for a in (lengths, order, queries, keys_values)
    ]
    return pl.pallas_call(
        kernel,
        out_shape=jax.ShapeDtypeStruct(queries.shape, queries.dtype),
        in_specs=[
            pl.BlockSpec(memory_space=pltpu.SMEM),
            pl.BlockSpec(memory_space=pltpu.SMEM),
            pl.BlockSpec(memory_space=pltpu.HBM),
            pl.BlockSpec(memory_space=pltpu.HBM),
        ],
        out_specs=pl.BlockSpec(memory_space=pl.ANY),
        scratch_shapes=[
            pltpu.VMEM((micro, tok, groups, pair), jnp.bfloat16),
            pltpu.VMEM((2, tok * groups, pair // 2), jnp.float32),
            pltpu.VMEM((chunks, keys, pair), jnp.bfloat16),
            pltpu.VMEM((micro, tok, q_cols), jnp.bfloat16),
            pltpu.VMEM((chunks, share // joint, tok, joint * head), jnp.bfloat16),
            pltpu.VMEM((micro, tok, keys), jnp.float32),
            pltpu.SemaphoreType.DMA((1 + micro,)),
            pltpu.SemaphoreType.DMA((reach + 1, chunks + 2)),
            pltpu.SemaphoreType.DMA((hops,)),
            pltpu.SemaphoreType.DMA((max(1, moves),)),
            pltpu.SemaphoreType.DMA(()),
            pltpu.SemaphoreType.DMA(()),
        ],
        compiler_params=pltpu.CompilerParams(
            collective_id=0,
            has_side_effects=True,
            vmem_limit_bytes=40 * 1024 * 1024,
        ),
        name="relay_attention",
    )(*inputs)


def solution(mesh):
    placed = (
        P("section", None, "seq", None),
        P("section", None, "seq", None, None),
        P("section", None, None),
        P("section", None),
    )
    return jax.shard_map(
        local,
        mesh=mesh,
        in_specs=placed,
        out_specs=P("section", None, "seq", None),
        check_vma=False,
    )
```
